32 devices in a mesh: sta: 8 (over z, y), win: 4 (over x, core).
Axes of the slice: x: 2, y: 2, z: 4, core: 2. Of those that a mesh axis runs over, the one named last changes fastest.
Arguments:
- spectra: bfloat16 [64, 56, 4096], P('win', 'sta'), may hold values from -6 to 6
- pair_bins: int32 [56, 3, 7], P('sta'), may hold values from 0 to 15
- owner_count: int32 [8], replicated, may hold values from 1 to 4, 16 in all
- bin_order: int32 [16], replicated, may hold values from 0 to 15, each once
Outputs:
- owned_stacks: float32 [32, 4096], P('sta', 'win')
The draws below stay inside these ranges and needn't reach their ends.
Inputs may be any that keep to these rules, and one draw needn't show every extreme that they name: Owner o holds owner_count[o] bins; the counts sum to 16 and the largest is exactly 4. `bin_order`: every bin appears exactly once.
All inputs are finite; a program needn't handle non-finite values.
Results may differ from the reference program's by a relative error of at most 0.0011.
Values may be sent and summed in bfloat16 or wider, within the bound.
A program may use at most 128 MiB of HBM per device.

```python
import math
import jax
import jax.numpy as jnp
import numpy as np
from jax import lax

F = 2048
S_DEV = 7
W_DEV = 16
ROUNDS = 3
CAP = 4
STATIONS = 56
NWIN = 64
NBINS = 16
N_STA = 8
N_WIN = 4


def place_ends(result, key, smallest, largest):
    shape = result.shape
    place = [jax.random.randint(jax.random.fold_in(key, axis), (), 0, shape[axis]) for axis in range(len(shape))]
    result = result.at[tuple(place)].set(smallest)
    longest = shape.index(max(shape))
    place[longest] = (place[longest] + 1) % shape[longest]
    return result.at[tuple(place)].set(largest)


def block_levels(stream_key, dims, split, least, top_value):
    loudness, own = 1.0, jax.random.fold_in(stream_key, 6)
    for dim, blocks in split:
        draws = jnp.exp(jax.random.uniform(jax.random.fold_in(own, dim), (blocks,), jnp.float32, least / len(split), top_value / len(split)))
        loudness = loudness * jnp.repeat(draws, dims[dim] // blocks).reshape([-1 if axis == dim else 1 for axis in range(len(dims))])
    return loudness


def profile(count, total, limit, slope):
    weights = [(1 << 20) // math.isqrt(rank ** slope) + 1 for rank in range(2, count + 1)]
    surplus, given = total - limit - (count - 1), [1] * (count - 1)
    while surplus > 0:
        movable = [i for i in range(count - 1) if given[i] < limit]
        whole, remaining = sum([weights[i] for i in movable]), surplus
        for i in movable:
            extra = min(limit - given[i], max(1, remaining * weights[i] // whole), surplus)
            given[i] = given[i] + extra
            surplus = surplus - extra
    return np.array([limit] + given)


def uneven_parts(key, amount, total, limit, slope):
    if amount == 2:
        one = jax.random.randint(key, (), max(1, total - limit), min(limit, total - 1) + 1)
        return jnp.stack([one, total - one])
    tallies = jnp.asarray(profile(amount, total, limit, slope), jnp.int32)
    twos = (amount - 1) // 2
    source_of, receiver = tallies[1:1 + 2 * twos:2], tallies[2:2 + 2 * twos:2]
    room = jnp.minimum(source_of - 1, limit - receiver)
    passed = jax.random.randint(jax.random.fold_in(key, 1), (twos,), 0, 1 << 20) % (room + 1)
    tallies = tallies.at[1:1 + 2 * twos:2].set(source_of - passed).at[2:2 + 2 * twos:2].set(receiver + passed)
    return tallies[jax.random.permutation(jax.random.fold_in(key, 2), amount)]


def normal_values(own_key, shape, scale, limit, cuts=(), kind=jnp.bfloat16):
    factor_of = block_levels(own_key, shape, cuts, -0.22, 0.18) if cuts else 1.0
    entries = jax.random.normal(own_key, shape, jnp.float32) * scale * factor_of
    return jnp.minimum(jnp.maximum(entries, -limit), limit).astype(kind)


def setup_inputs(seed: int = 0) -> dict:
    streams_of = jax.random.split(jax.random.key(seed), 5)
    return {
        "spectra": normal_values(streams_of[0], (NWIN, STATIONS, 2 * F), 1.0, 6.0, ((0, 4), (1, 8))),
        "pair_bins": place_ends(jax.random.randint(streams_of[1], (STATIONS, ROUNDS, S_DEV), 0, NBINS), jax.random.fold_in(streams_of[1], 1), 0, NBINS - 1).astype(jnp.int32),
        "owner_count": uneven_parts(streams_of[2], N_STA, NBINS, CAP, 2).astype(jnp.int32),
        "bin_order": jax.random.permutation(streams_of[3], NBINS).astype(jnp.int32),
    }


def cross_all(own, other):
    width = own.shape[-1] // 2
    own_re, own_im = own[..., :width], own[..., width:]
    other_re, other_im = other[..., :width], other[..., width:]
    form = "gwsf,gwtf->gstf"
    real = jnp.einsum(form, own_re, other_re, precision=lax.Precision.HIGHEST) + jnp.einsum(form, own_im, other_im, precision=lax.Precision.HIGHEST)
    imag = jnp.einsum(form, own_im, other_re, precision=lax.Precision.HIGHEST) - jnp.einsum(form, own_re, other_im, precision=lax.Precision.HIGHEST)
    return jnp.concatenate([real, imag], axis=-1)


def reference(spectra, pair_bins, owner_count, bin_order):
    shaped = spectra.reshape(N_WIN, W_DEV, N_STA, S_DEV, 2 * F)
    bins_shaped = pair_bins.reshape(N_STA, S_DEV, ROUNDS, S_DEV)

    def per_block(totals, block):
        own = lax.dynamic_index_in_dim(shaped, block, 2, keepdims=False).astype(jnp.float32)
        labels_all = lax.dynamic_index_in_dim(bins_shaped, block, 0, keepdims=False)
        for offset in range(ROUNDS):
            partner = ((block - offset) % N_STA).astype(jnp.int32)
            other = lax.dynamic_index_in_dim(shaped, partner, 2, keepdims=False).astype(jnp.float32)
            crossed = cross_all(own, other)
            rounded = lax.optimization_barrier(crossed.astype(jnp.bfloat16)).astype(jnp.float32)
            labels = jnp.broadcast_to(labels_all[:, offset, :], (N_WIN, S_DEV, S_DEV)).reshape(-1)
            totals = totals + jax.ops.segment_sum(rounded.reshape(-1, 2 * F), labels, num_segments=NBINS)
        return totals, None

    totals, _ = lax.scan(per_block, jnp.zeros((NBINS, 2 * F), jnp.float32), jnp.arange(N_STA, dtype=jnp.int32))
    starts = (jnp.cumsum(owner_count) - owner_count).astype(jnp.int32)
    ranks = jnp.arange(CAP, dtype=jnp.int32)
    positions = jnp.clip(starts[:, None] + ranks[None, :], 0, NBINS - 1).astype(jnp.int32)
    valid = ranks[None, :] < owner_count[:, None]
    chosen = bin_order[positions]
    stacks = jnp.where(valid[..., None], totals[chosen], jnp.float32(0.0))
    return stacks.reshape(N_STA * CAP, 2 * F) * jnp.float32(1.0 / NWIN)
```

```python
import functools
import jax
import jax.numpy as jnp
from jax import lax
from jax.experimental import pallas as pl
from jax.experimental.pallas import tpu as pltpu
from jax.sharding import PartitionSpec as P

CAP = 4
LANES = 128
ROWS = 8
MESH = pl.DeviceIdType.MESH


def passed_along(value, axis, steps):
    count = lax.axis_size(axis)
    pairs = [(source, (source + steps) % count) for source in range(count)]
    return lax.ppermute(value, axis, pairs)


def cross_pairs(own, other):
    width = own.shape[-1] // 2
    own_re, own_im = (own[..., :width], own[..., width:])
    other_re, other_im = (other[..., :width], other[..., width:])
    form = "wsf,wtf->stf"
    real = jnp.einsum(form, own_re, other_re, preferred_element_type=jnp.float32) + jnp.einsum(
        form, own_im, other_im, preferred_element_type=jnp.float32
    )
    imag = jnp.einsum(form, own_im, other_re, preferred_element_type=jnp.float32) - jnp.einsum(
        form, own_re, other_im, preferred_element_type=jnp.float32
    )
    joined = jnp.concatenate([real, imag], axis=-1).astype(jnp.bfloat16)
    return joined.reshape(-1, joined.shape[-1])


def by_blocks(spectra, pair_bins, owner_count, bin_order):
    rounds = pair_bins.shape[1]
    blocks = [spectra]
    for offset in range(1, rounds):
        blocks.append(passed_along(spectra, "sta", offset))
    crossed = jnp.concatenate([cross_pairs(spectra, other) for other in blocks], axis=0)
    labels = jnp.transpose(pair_bins, (1, 0, 2)).reshape(-1)
    bin_total = bin_order.shape[0]
    starts = jnp.cumsum(owner_count) - owner_count
    ranks = jnp.arange(CAP, dtype=jnp.int32)
    positions = jnp.clip(starts[:, None] + ranks[None, :], 0, bin_total - 1)
    valid = ranks[None, :] < owner_count[:, None]
    chosen = jnp.take(bin_order, positions)
    slot_bin = jnp.where(valid, chosen, -1).reshape(-1)
    window_total = spectra.shape[0] * lax.axis_size("win")
    matches = (slot_bin[:, None] == labels[None, :]).astype(jnp.bfloat16)
    partial_sums = jnp.dot(matches, crossed, preferred_element_type=jnp.float32)
    spread = lax.psum_scatter(partial_sums, "win", scatter_dimension=1, tiled=True)
    stacks = lax.psum_scatter(spread, "sta", scatter_dimension=0, tiled=True)
    return stacks * jnp.float32(1.0 / window_total)


def kernel(
    sizes, spec_ref, bins_ref, count_ref, order_ref, out_ref,
    recv, wide, lab, slots, crossed, total, outbox, inbox,
    send_sem, recv_sem, own_sem, lab_send, lab_recv, box_send, box_recv,
):
    n_sta, n_win, chunks, windows, stations, rounds, width = sizes
    share = width // n_sta
    out_cols = out_ref.shape[1]
    per_out = out_cols // share
    halves = width // out_cols
    me = lax.axis_index("sta")
    g = lax.axis_index("win")

    barrier = pltpu.get_barrier_semaphore()
    for t in range(1, n_sta * n_win):
        flat = lax.rem(me * n_win + g + t, n_sta * n_win)
        pl.semaphore_signal(
            barrier, inc=1, device_id=(flat // n_win, lax.rem(flat, n_win)), device_id_type=MESH
        )
    pl.semaphore_wait(barrier, n_sta * n_win - 1)

    def share_of(dest, c, part):
        col = pl.multiple_of(part * width + dest * share + c * LANES, LANES)
        return spec_ref.at[:, :, pl.ds(col, LANES)]

    def spectra_copy(c, k, part):
        dest = lax.rem(me + k, n_sta)
        return pltpu.make_async_remote_copy(
            src_ref=share_of(dest, c, part),
            dst_ref=recv.at[c, me, part],
            send_sem=send_sem.at[c, k, part],
            recv_sem=recv_sem.at[c, me, part],
            device_id=(dest, g),
            device_id_type=MESH,
        )

    def own_copy(c, part):
        return pltpu.make_async_copy(share_of(me, c, part), recv.at[c, me, part], own_sem.at[c, part])

    for c in range(chunks):
        for k in range(1, n_sta):
            for part in range(2):
                spectra_copy(c, k, part).start()
        for part in range(2):
            own_copy(c, part).start()

    lane = lax.broadcasted_iota(jnp.int32, (1, lab.shape[2]), 1)
    row = jnp.full((1, lab.shape[2]), -2, jnp.int32)
    for r in range(rounds):
        for j in range(stations):
            for i in range(stations):
                row = jnp.where(lane == (r * ROWS + j) * ROWS + i, bins_ref[r, i, j], row)
    lab[pl.ds(me, 1)] = row[None]

    def label_copy(k):
        return pltpu.make_async_remote_copy(
            src_ref=lab.at[me],
            dst_ref=lab.at[me],
            send_sem=lab_send.at[k],
            recv_sem=lab_recv.at[me],
            device_id=(lax.rem(me + k, n_sta), g),
            device_id_type=MESH,
        )

    for k in range(1, n_sta):
        label_copy(k).start()

    sub = lax.broadcasted_iota(jnp.int32, (n_sta * CAP, LANES), 0)
    slot = jnp.full((n_sta * CAP, LANES), -1, jnp.int32)
    start = jnp.int32(0)
    for o in range(n_sta):
        held = count_ref[o]
        for k in range(CAP):
            chosen = order_ref[jnp.clip(start + k, 0, order_ref.shape[0] - 1)]
            slot = jnp.where(sub == o * CAP + k, jnp.where(k < held, chosen, -1), slot)
        start = start + held
    slots[...] = slot

    wide[...] = jnp.zeros_like(wide)
    crossed[...] = jnp.zeros_like(crossed)
    for k in range(1, n_sta):
        src = lax.rem(me - k + n_sta, n_sta)
        pltpu.make_async_remote_copy(
            src_ref=lab.at[src], dst_ref=lab.at[src], send_sem=lab_send.at[k],
            recv_sem=lab_recv.at[src], device_id=(src, g), device_id_type=MESH,
        ).wait_recv()

    def widen(c, p):
        for part in range(2):
            for j in range(stations):
                wide[p, part, pl.ds(j, windows, stride=ROWS), :] = recv[c, p, part, j].astype(jnp.float32)

    def arrive(c, k):
        src = lax.rem(me - k + n_sta, n_sta)
        for part in range(2):
            pltpu.make_async_remote_copy(
                src_ref=recv.at[c, src, part], dst_ref=recv.at[c, src, part],
                send_sem=send_sem.at[c, k, part], recv_sem=recv_sem.at[c, src, part],
                device_id=(src, g), device_id_type=MESH,
            ).wait_recv()
        widen(c, src)

    def step(p):
        blocks = [lax.rem(p + r, n_sta) for r in range(rounds)]
        re = [[None] * stations for _ in range(rounds)]
        im = [[None] * stations for _ in range(rounds)]
        for w in range(windows):
            at = pl.ds(w * ROWS, ROWS)
            mine = [(wide[b, 0, at, :], wide[b, 1, at, :]) for b in blocks]
            for j in range(stations):
                a = jnp.broadcast_to(wide[p, 0, pl.ds(w * ROWS + j, 1), :], (ROWS, LANES))
                b = jnp.broadcast_to(wide[p, 1, pl.ds(w * ROWS + j, 1), :], (ROWS, LANES))
                for r in range(rounds):
                    x, y = mine[r]
                    if w == 0:
                        re[r][j] = x * a + y * b
                        im[r][j] = y * a - x * b
                    else:
                        re[r][j] = re[r][j] + x * a + y * b
                        im[r][j] = im[r][j] + y * a - x * b
        blank = jnp.zeros((ROWS, LANES), jnp.float32)
        for r in range(rounds):
            at = pl.ds(r * ROWS * ROWS, ROWS * ROWS)
            pad = [blank] * (ROWS - stations)
            crossed[at, 0:LANES] = jnp.concatenate(re[r] + pad, axis=0).astype(jnp.bfloat16)
            crossed[at, LANES:] = jnp.concatenate(im[r] + pad, axis=0).astype(jnp.bfloat16)
        lanes = lax.broadcasted_iota(jnp.int32, (1, lab.shape[2]), 1)
        names = jnp.full((1, lab.shape[2]), -2, jnp.int32)
        for r in range(rounds):
            names = jnp.where(lanes // (ROWS * ROWS) == r, lab[blocks[r]], names)
        match = jnp.concatenate(
            [slots[...] == names[:, at:at + LANES] for at in range(0, lab.shape[2], LANES)], axis=1
        )
        match = jnp.where(match, 1.0, 0.0).astype(jnp.bfloat16)
        return jnp.dot(match, crossed[...], preferred_element_type=jnp.float32)

    def box_copies(c, o, part):
        q = part * halves + me // per_out
        t = lax.rem(me, per_out)
        col = pl.multiple_of(t * share + c * LANES, LANES)
        src = outbox.at[c, part, o]
        dst = inbox.at[g, :, pl.ds(col, LANES)]

        def far():
            return pltpu.make_async_remote_copy(
                src_ref=src, dst_ref=dst, send_sem=box_send.at[c, part, o],
                recv_sem=box_recv.at[c, t, g], device_id=(o, q), device_id_type=MESH,
            )

        def near():
            return pltpu.make_async_copy(src, dst, box_recv.at[c, t, g])

        return far, near, jnp.logical_and(o == me, q == g)

    def one_chunk(c, carry):
        for part in range(2):
            own_copy(c, part).wait()
        widen(c, me)
        arrive(c, 1)
        total[...] = jnp.zeros_like(total)

        def one_step(k, carry):
            @pl.when(k < n_sta)
            def _():
                arrive(c, k)

            total[...] += step(lax.rem(me - k + 2 * n_sta, n_sta))
            return carry

        lax.fori_loop(rounds - 1, n_sta + rounds - 1, one_step, 0)
        for part in range(2):
            for o in range(n_sta):
                outbox[c, part, o] = total[o * CAP:(o + 1) * CAP, part * LANES:(part + 1) * LANES]
        for part in range(2):
            for o in range(n_sta):
                far, near, is_me = box_copies(c, o, part)
                pl.when(is_me)(lambda near=near: near().start())
                pl.when(jnp.logical_not(is_me))(lambda far=far: far().start())
        return carry

    lax.fori_loop(0, chunks, one_chunk, 0)

    for c in range(chunks):
        for t in range(per_out):
            for s in range(n_win):
                dst = inbox.at[s, :, pl.ds(t * share + c * LANES, LANES)]
                pltpu.make_async_copy(dst, dst, box_recv.at[c, t, s]).wait()
    out_ref[...] = functools.reduce(jnp.add, [inbox[s] for s in range(n_win)])

    for c in range(chunks):
        for k in range(1, n_sta):
            for part in range(2):
                spectra_copy(c, k, part).wait_send()
        for part in range(2):
            for o in range(n_sta):
                far, near, is_me = box_copies(c, o, part)
                pl.when(jnp.logical_not(is_me))(lambda far=far: far().wait_send())
    for k in range(1, n_sta):
        label_copy(k).wait_send()


def by_frequency(spectra, pair_bins, owner_count, bin_order):
    n_sta, n_win = lax.axis_size("sta"), lax.axis_size("win")
    windows, stations, columns = spectra.shape
    rounds = pair_bins.shape[1]
    width = columns // 2
    share = width // n_sta
    chunks = share // LANES
    out_cols = columns // n_win
    per_out = out_cols // share
    depth = -(-rounds * ROWS * ROWS // LANES) * LANES
    sizes = (n_sta, n_win, chunks, windows, stations, rounds, width)
    dma = pltpu.SemaphoreType.DMA
    sums = pl.pallas_call(
        functools.partial(kernel, sizes),
        out_shape=jax.ShapeDtypeStruct((CAP, out_cols), jnp.float32),
        in_specs=[
            pl.BlockSpec(memory_space=pl.ANY),
            pl.BlockSpec(memory_space=pltpu.SMEM),
            pl.BlockSpec(memory_space=pltpu.SMEM),
            pl.BlockSpec(memory_space=pltpu.SMEM),
        ],
        out_specs=pl.BlockSpec(memory_space=pltpu.VMEM),
        scratch_shapes=[
            pltpu.VMEM((chunks, n_sta, 2, stations, windows, LANES), spectra.dtype),
            pltpu.VMEM((n_sta, 2, windows * ROWS, LANES), jnp.float32),
            pltpu.VMEM((n_sta, 1, depth), jnp.int32),
            pltpu.VMEM((n_sta * CAP, LANES), jnp.int32),
            pltpu.VMEM((depth, 2 * LANES), jnp.bfloat16),
            pltpu.VMEM((n_sta * CAP, 2 * LANES), jnp.float32),
            pltpu.VMEM((chunks, 2, n_sta, CAP, LANES), jnp.float32),
            pltpu.VMEM((n_win, CAP, out_cols), jnp.float32),
            dma((chunks, n_sta, 2)),
            dma((chunks, n_sta, 2)),
            dma((chunks, 2)),
            dma((n_sta,)),
            dma((n_sta,)),
            dma((chunks, 2, n_sta)),
            dma((chunks, per_out, n_win)),
        ],
        compiler_params=pltpu.CompilerParams(
            collective_id=0, has_side_effects=True, vmem_limit_bytes=56 * 1024 * 1024
        ),
        cost_estimate=pl.CostEstimate(
            flops=8 * width * windows * rounds * stations * stations,
            bytes_accessed=2 * spectra.size, transcendentals=0,
        ),
    )(jnp.transpose(spectra, (1, 0, 2)), jnp.transpose(pair_bins, (1, 0, 2)), owner_count, bin_order)
    return sums * jnp.float32(1.0 / (windows * n_win))


def on_device(spectra, pair_bins, owner_count, bin_order):
    n_sta, n_win = lax.axis_size("sta"), lax.axis_size("win")
    width = spectra.shape[2] // 2
    share, out_cols = width // n_sta, 2 * width // n_win
    fits = (
        width % (n_sta * LANES) == 0 and out_cols % share == 0 and width % out_cols == 0
        and spectra.shape[1] <= ROWS and pair_bins.shape[1] <= n_sta - 1
    )
    plan = by_frequency if fits else by_blocks
    return plan(spectra, pair_bins, owner_count, bin_order)


def solution(mesh):
    return jax.shard_map(
        on_device,
        mesh=mesh,
        in_specs=(P("win", "sta", None), P("sta", None, None), P(), P()),
        out_specs=P("sta", "win"),
        check_vma=False,
    )
```

```python
import functools
import jax
import jax.numpy as jnp
from jax import lax
from jax.experimental import pallas as pl
from jax.experimental.pallas import tpu as pltpu
from jax.sharding import PartitionSpec as P

CAP = 4
LANES = 128
ROWS = 8
MESH = pl.DeviceIdType.MESH


def passed_along(value, axis, steps):
    count = lax.axis_size(axis)
    pairs = [(source, (source + steps) % count) for source in range(count)]
    return lax.ppermute(value, axis, pairs)


def cross_pairs(own, other):
    width = own.shape[-1] // 2
    own_re, own_im = (own[..., :width], own[..., width:])
    other_re, other_im = (other[..., :width], other[..., width:])
    form = "wsf,wtf->stf"
    real = jnp.einsum(form, own_re, other_re, preferred_element_type=jnp.float32) + jnp.einsum(
        form, own_im, other_im, preferred_element_type=jnp.float32
    )
    imag = jnp.einsum(form, own_im, other_re, preferred_element_type=jnp.float32) - jnp.einsum(
        form, own_re, other_im, preferred_element_type=jnp.float32
    )
    joined = jnp.concatenate([real, imag], axis=-1).astype(jnp.bfloat16)
    return joined.reshape(-1, joined.shape[-1])


def by_blocks(spectra, pair_bins, owner_count, bin_order):
    rounds = pair_bins.shape[1]
    blocks = [spectra]
    for offset in range(1, rounds):
        blocks.append(passed_along(spectra, "sta", offset))
    crossed = jnp.concatenate([cross_pairs(spectra, other) for other in blocks], axis=0)
    labels = jnp.transpose(pair_bins, (1, 0, 2)).reshape(-1)
    bin_total = bin_order.shape[0]
    starts = jnp.cumsum(owner_count) - owner_count
    ranks = jnp.arange(CAP, dtype=jnp.int32)
    positions = jnp.clip(starts[:, None] + ranks[None, :], 0, bin_total - 1)
    valid = ranks[None, :] < owner_count[:, None]
    chosen = jnp.take(bin_order, positions)
    slot_bin = jnp.where(valid, chosen, -1).reshape(-1)
    window_total = spectra.shape[0] * lax.axis_size("win")
    matches = (slot_bin[:, None] == labels[None, :]).astype(jnp.bfloat16)
    partial_sums = jnp.dot(matches, crossed, preferred_element_type=jnp.float32)
    spread = lax.psum_scatter(partial_sums, "win", scatter_dimension=1, tiled=True)
    stacks = lax.psum_scatter(spread, "sta", scatter_dimension=0, tiled=True)
    return stacks * jnp.float32(1.0 / window_total)


def kernel(
    sizes, spec_ref, bins_ref, count_ref, order_ref, out_ref,
    recv, wide, lab, slots, crossed, total, outbox, inbox,
    send_sem, recv_sem, own_sem, lab_send, lab_recv, box_send, box_recv,
):
    n_sta, n_win, chunks, windows, stations, rounds, width = sizes
    share = width // n_sta
    out_cols = out_ref.shape[1]
    per_out = out_cols // share
    halves = width // out_cols
    me = lax.axis_index("sta")
    g = lax.axis_index("win")

    barrier = pltpu.get_barrier_semaphore()
    for t in range(1, n_sta * n_win):
        flat = lax.rem(me * n_win + g + t, n_sta * n_win)
        pl.semaphore_signal(
            barrier, inc=1, device_id=(flat // n_win, lax.rem(flat, n_win)), device_id_type=MESH
        )
    pl.semaphore_wait(barrier, n_sta * n_win - 1)

    def partner(k):
        if n_sta & (n_sta - 1):
            return lax.rem(me + k, n_sta)
        digits, bit = me, 1
        while bit < n_sta:
            if k & bit:
                digits = digits + bit - 2 * bit * lax.rem(digits // bit, 2)
            bit *= 2
        return digits

    far_half = list(range(n_sta // 2, n_sta))
    near_half = list(range(1, n_sta // 2)) + [None]
    turns = [k for pair in zip(far_half, near_half) for k in pair if k is not None]

    def share_of(dest, c, part):
        col = pl.multiple_of(part * width + dest * share + c * LANES, LANES)
        return spec_ref.at[:, :, pl.ds(col, LANES)]

    def spectra_copy(c, k, part):
        dest = partner(k)
        return pltpu.make_async_remote_copy(
            src_ref=share_of(dest, c, part),
            dst_ref=recv.at[c, me, part],
            send_sem=send_sem.at[c, k, part],
            recv_sem=recv_sem.at[c, me, part],
            device_id=(dest, g),
            device_id_type=MESH,
        )

    def own_copy(c, part):
        return pltpu.make_async_copy(share_of(me, c, part), recv.at[c, me, part], own_sem.at[c, part])

    for c in range(chunks):
        for part in range(2):
            own_copy(c, part).start()
    for k in turns:
        for part in range(2):
            spectra_copy(0, k, part).start()

    lane = lax.broadcasted_iota(jnp.int32, (1, lab.shape[2]), 1)
    row = jnp.full((1, lab.shape[2]), -2, jnp.int32)
    for r in range(rounds):
        for j in range(stations):
            for i in range(stations):
                row = jnp.where(lane == (r * ROWS + j) * ROWS + i, bins_ref[r, i, j], row)
    lab[pl.ds(me, 1)] = row[None]

    def label_copy(k):
        return pltpu.make_async_remote_copy(
            src_ref=lab.at[me],
            dst_ref=lab.at[me],
            send_sem=lab_send.at[k],
            recv_sem=lab_recv.at[me],
            device_id=(lax.rem(me + k, n_sta), g),
            device_id_type=MESH,
        )

    for k in range(1, n_sta):
        label_copy(k).start()

    sub = lax.broadcasted_iota(jnp.int32, (n_sta * CAP, LANES), 0)
    slot = jnp.full((n_sta * CAP, LANES), -1, jnp.int32)
    start = jnp.int32(0)
    for o in range(n_sta):
        held = count_ref[o]
        for k in range(CAP):
            chosen = order_ref[jnp.clip(start + k, 0, order_ref.shape[0] - 1)]
            slot = jnp.where(sub == o * CAP + k, jnp.where(k < held, chosen, -1), slot)
        start = start + held
    slots[...] = slot

    wide[...] = jnp.zeros_like(wide)
    crossed[...] = jnp.zeros_like(crossed)
    for k in range(1, n_sta):
        src = lax.rem(me - k + n_sta, n_sta)
        pltpu.make_async_remote_copy(
            src_ref=lab.at[src], dst_ref=lab.at[src], send_sem=lab_send.at[k],
            recv_sem=lab_recv.at[src], device_id=(src, g), device_id_type=MESH,
        ).wait_recv()

    for c in range(1, chunks):
        for k in turns:
            for part in range(2):
                spectra_copy(c - 1, k, part).wait_send()
                spectra_copy(c, k, part).start()

    def widen(c, p):
        for part in range(2):
            for j in range(stations):
                wide[p, part, pl.ds(j, windows, stride=ROWS), :] = recv[c, p, part, j].astype(jnp.float32)

    def arrive(c, k):
        src = lax.rem(me - k + n_sta, n_sta)
        for part in range(2):
            pltpu.make_async_remote_copy(
                src_ref=recv.at[c, src, part], dst_ref=recv.at[c, src, part],
                send_sem=send_sem.at[c, k, part], recv_sem=recv_sem.at[c, src, part],
                device_id=(src, g), device_id_type=MESH,
            ).wait_recv()
        widen(c, src)

    def step(p):
        blocks = [lax.rem(p + r, n_sta) for r in range(rounds)]
        re = [[None] * stations for _ in range(rounds)]
        im = [[None] * stations for _ in range(rounds)]
        half = -(-stations // 2)
        for group in (range(half), range(half, stations)):
            for w in range(windows):
                at = pl.ds(w * ROWS, ROWS)
                mine = [(wide[b, 0, at, :], wide[b, 1, at, :]) for b in blocks]
                for j in group:
                    a = wide[p, 0, pl.ds(w * ROWS + j, ROWS, stride=0), :]
                    b = wide[p, 1, pl.ds(w * ROWS + j, ROWS, stride=0), :]
                    for r in range(rounds):
                        x, y = mine[r]
                        if w == 0:
                            re[r][j] = x * a + y * b
                            im[r][j] = y * a - x * b
                        else:
                            re[r][j] = re[r][j] + x * a + y * b
                            im[r][j] = im[r][j] + y * a - x * b
        blank = jnp.zeros((ROWS, LANES), jnp.float32)
        for r in range(rounds):
            at = pl.ds(r * ROWS * ROWS, ROWS * ROWS)
            pad = [blank] * (ROWS - stations)
            crossed[at, 0:LANES] = jnp.concatenate(re[r] + pad, axis=0).astype(jnp.bfloat16)
            crossed[at, LANES:] = jnp.concatenate(im[r] + pad, axis=0).astype(jnp.bfloat16)
        lanes = lax.broadcasted_iota(jnp.int32, (1, lab.shape[2]), 1)
        names = jnp.full((1, lab.shape[2]), -2, jnp.int32)
        for r in range(rounds):
            names = jnp.where(lanes // (ROWS * ROWS) == r, lab[blocks[r]], names)
        match = jnp.concatenate(
            [slots[...] == names[:, at:at + LANES] for at in range(0, lab.shape[2], LANES)], axis=1
        )
        match = jnp.where(match, 1.0, 0.0).astype(jnp.bfloat16)
        return jnp.dot(match, crossed[...], preferred_element_type=jnp.float32)

    def box_copies(c, o, part):
        q = part * halves + me // per_out
        t = lax.rem(me, per_out)
        col = pl.multiple_of(t * share + c * LANES, LANES)
        src = outbox.at[c, part, o]
        dst = inbox.at[g, :, pl.ds(col, LANES)]

        def far():
            return pltpu.make_async_remote_copy(
                src_ref=src, dst_ref=dst, send_sem=box_send.at[c, part, o],
                recv_sem=box_recv.at[c, t, g], device_id=(o, q), device_id_type=MESH,
            )

        def near():
            return pltpu.make_async_copy(src, dst, box_recv.at[c, t, g])

        return far, near, jnp.logical_and(o == me, q == g)

    def one_chunk(c, carry):
        for part in range(2):
            own_copy(c, part).wait()
        widen(c, me)
        arrive(c, 1)
        total[...] = jnp.zeros_like(total)

        def one_step(k, carry):
            @pl.when(k < n_sta)
            def _():
                arrive(c, k)

            total[...] += step(lax.rem(me - k + 2 * n_sta, n_sta))
            return carry

        lax.fori_loop(rounds - 1, n_sta + rounds - 1, one_step, 0)
        for part in range(2):
            for o in range(n_sta):
                outbox[c, part, o] = total[o * CAP:(o + 1) * CAP, part * LANES:(part + 1) * LANES]
        for part in range(2):
            for o in range(n_sta):
                far, near, is_me = box_copies(c, o, part)
                pl.when(is_me)(lambda near=near: near().start())
                pl.when(jnp.logical_not(is_me))(lambda far=far: far().start())
        return carry

    lax.fori_loop(0, chunks, one_chunk, 0)

    for c in range(chunks):
        for t in range(per_out):
            for s in range(n_win):
                dst = inbox.at[s, :, pl.ds(t * share + c * LANES, LANES)]
                pltpu.make_async_copy(dst, dst, box_recv.at[c, t, s]).wait()
    out_ref[...] = functools.reduce(jnp.add, [inbox[s] for s in range(n_win)])

    for k in turns:
        for part in range(2):
            spectra_copy(chunks - 1, k, part).wait_send()
    for c in range(chunks):
        for part in range(2):
            for o in range(n_sta):
                far, near, is_me = box_copies(c, o, part)
                pl.when(jnp.logical_not(is_me))(lambda far=far: far().wait_send())
    for k in range(1, n_sta):
        label_copy(k).wait_send()


def by_frequency(spectra, pair_bins, owner_count, bin_order):
    n_sta, n_win = lax.axis_size("sta"), lax.axis_size("win")
    windows, stations, columns = spectra.shape
    rounds = pair_bins.shape[1]
    width = columns // 2
    share = width // n_sta
    chunks = share // LANES
    out_cols = columns // n_win
    per_out = out_cols // share
    depth = -(-rounds * ROWS * ROWS // LANES) * LANES
    sizes = (n_sta, n_win, chunks, windows, stations, rounds, width)
    dma = pltpu.SemaphoreType.DMA
    sums = pl.pallas_call(
        functools.partial(kernel, sizes),
        out_shape=jax.ShapeDtypeStruct((CAP, out_cols), jnp.float32),
        in_specs=[
            pl.BlockSpec(memory_space=pl.ANY),
            pl.BlockSpec(memory_space=pltpu.SMEM),
            pl.BlockSpec(memory_space=pltpu.SMEM),
            pl.BlockSpec(memory_space=pltpu.SMEM),
        ],
        out_specs=pl.BlockSpec(memory_space=pltpu.VMEM),
        scratch_shapes=[
            pltpu.VMEM((chunks, n_sta, 2, stations, windows, LANES), spectra.dtype),
            pltpu.VMEM((n_sta, 2, windows * ROWS, LANES), jnp.float32),
            pltpu.VMEM((n_sta, 1, depth), jnp.int32),
            pltpu.VMEM((n_sta * CAP, LANES), jnp.int32),
            pltpu.VMEM((depth, 2 * LANES), jnp.bfloat16),
            pltpu.VMEM((n_sta * CAP, 2 * LANES), jnp.float32),
            pltpu.VMEM((chunks, 2, n_sta, CAP, LANES), jnp.float32),
            pltpu.VMEM((n_win, CAP, out_cols), jnp.float32),
            dma((chunks, n_sta, 2)),
            dma((chunks, n_sta, 2)),
            dma((chunks, 2)),
            dma((n_sta,)),
            dma((n_sta,)),
            dma((chunks, 2, n_sta)),
            dma((chunks, per_out, n_win)),
        ],
        compiler_params=pltpu.CompilerParams(
            collective_id=0, has_side_effects=True, vmem_limit_bytes=56 * 1024 * 1024
        ),
        cost_estimate=pl.CostEstimate(
            flops=8 * width * windows * rounds * stations * stations,
            bytes_accessed=2 * spectra.size, transcendentals=0,
        ),
    )(jnp.transpose(spectra, (1, 0, 2)), jnp.transpose(pair_bins, (1, 0, 2)), owner_count, bin_order)
    return sums * jnp.float32(1.0 / (windows * n_win))


def on_device(spectra, pair_bins, owner_count, bin_order):
    n_sta, n_win = lax.axis_size("sta"), lax.axis_size("win")
    width = spectra.shape[2] // 2
    share, out_cols = width // n_sta, 2 * width // n_win
    fits = (
        width % (n_sta * LANES) == 0 and out_cols % share == 0 and width % out_cols == 0
        and spectra.shape[1] <= ROWS and pair_bins.shape[1] <= n_sta - 1
    )
    plan = by_frequency if fits else by_blocks
    return plan(spectra, pair_bins, owner_count, bin_order)


def solution(mesh):
    return jax.shard_map(
        on_device,
        mesh=mesh,
        in_specs=(P("win", "sta", None), P("sta", None, None), P(), P()),
        out_specs=P("sta", "win"),
        check_vma=False,
    )
```

```python
import functools
import jax
import jax.numpy as jnp
from jax import lax
from jax.experimental import pallas as pl
from jax.experimental.pallas import tpu as pltpu
from jax.sharding import PartitionSpec as P

CAP = 4
LANES = 128
ROWS = 8
MESH = pl.DeviceIdType.MESH


def passed_along(value, axis, steps):
    count = lax.axis_size(axis)
    pairs = [(source, (source + steps) % count) for source in range(count)]
    return lax.ppermute(value, axis, pairs)


def cross_pairs(own, other):
    width = own.shape[-1] // 2
    own_re, own_im = (own[..., :width], own[..., width:])
    other_re, other_im = (other[..., :width], other[..., width:])
    form = "wsf,wtf->stf"
    real = jnp.einsum(form, own_re, other_re, preferred_element_type=jnp.float32) + jnp.einsum(
        form, own_im, other_im, preferred_element_type=jnp.float32
    )
    imag = jnp.einsum(form, own_im, other_re, preferred_element_type=jnp.float32) - jnp.einsum(
        form, own_re, other_im, preferred_element_type=jnp.float32
    )
    joined = jnp.concatenate([real, imag], axis=-1).astype(jnp.bfloat16)
    return joined.reshape(-1, joined.shape[-1])


def by_blocks(spectra, pair_bins, owner_count, bin_order):
    rounds = pair_bins.shape[1]
    blocks = [spectra]
    for offset in range(1, rounds):
        blocks.append(passed_along(spectra, "sta", offset))
    crossed = jnp.concatenate([cross_pairs(spectra, other) for other in blocks], axis=0)
    labels = jnp.transpose(pair_bins, (1, 0, 2)).reshape(-1)
    bin_total = bin_order.shape[0]
    starts = jnp.cumsum(owner_count) - owner_count
    ranks = jnp.arange(CAP, dtype=jnp.int32)
    positions = jnp.clip(starts[:, None] + ranks[None, :], 0, bin_total - 1)
    valid = ranks[None, :] < owner_count[:, None]
    chosen = jnp.take(bin_order, positions)
    slot_bin = jnp.where(valid, chosen, -1).reshape(-1)
    window_total = spectra.shape[0] * lax.axis_size("win")
    matches = (slot_bin[:, None] == labels[None, :]).astype(jnp.bfloat16)
    partial_sums = jnp.dot(matches, crossed, preferred_element_type=jnp.float32)
    spread = lax.psum_scatter(partial_sums, "win", scatter_dimension=1, tiled=True)
    stacks = lax.psum_scatter(spread, "sta", scatter_dimension=0, tiled=True)
    return stacks * jnp.float32(1.0 / window_total)


def kernel(
    sizes, spec_ref, bins_ref, count_ref, order_ref, out_ref,
    recv, wide, lab, slots, crossed, total, outbox, inbox,
    send_sem, recv_sem, own_sem, lab_send, lab_recv, box_send, box_recv,
):
    n_sta, n_win, chunks, windows, stations, rounds, width = sizes
    share = width // n_sta
    out_cols = out_ref.shape[1]
    per_out = out_cols // share
    halves = width // out_cols
    me = lax.axis_index("sta")
    g = lax.axis_index("win")

    barrier = pltpu.get_barrier_semaphore()
    for t in range(1, n_sta * n_win):
        flat = lax.rem(me * n_win + g + t, n_sta * n_win)
        pl.semaphore_signal(
            barrier, inc=1, device_id=(flat // n_win, lax.rem(flat, n_win)), device_id_type=MESH
        )
    pl.semaphore_wait(barrier, n_sta * n_win - 1)

    def partner(k):
        if n_sta & (n_sta - 1):
            return lax.rem(me + k, n_sta)
        digits, bit = me, 1
        while bit < n_sta:
            if k & bit:
                digits = digits + bit - 2 * bit * lax.rem(digits // bit, 2)
            bit *= 2
        return digits

    far_half = list(range(n_sta // 2, n_sta))
    near_half = list(range(1, n_sta // 2)) + [None]
    turns = [k for pair in zip(far_half, near_half) for k in pair if k is not None]

    def share_of(dest, c, part):
        col = pl.multiple_of(part * width + dest * share + c * LANES, LANES)
        return spec_ref.at[:, :, pl.ds(col, LANES)]

    def spectra_copy(c, k, part):
        dest = partner(k)
        return pltpu.make_async_remote_copy(
            src_ref=share_of(dest, c, part),
            dst_ref=recv.at[c, me, part],
            send_sem=send_sem.at[c, k, part],
            recv_sem=recv_sem.at[c, me, part],
            device_id=(dest, g),
            device_id_type=MESH,
        )

    def own_copy(c, part):
        return pltpu.make_async_copy(share_of(me, c, part), recv.at[c, me, part], own_sem.at[c, part])

    for c in range(chunks):
        for part in range(2):
            own_copy(c, part).start()
    for k in turns:
        for part in range(2):
            spectra_copy(0, k, part).start()

    lane = lax.broadcasted_iota(jnp.int32, (1, lab.shape[2]), 1)
    row = jnp.full((1, lab.shape[2]), -2, jnp.int32)
    for r in range(rounds):
        for j in range(stations):
            for i in range(stations):
                row = jnp.where(lane == (r * ROWS + j) * ROWS + i, bins_ref[r, i, j], row)
    lab[pl.ds(me, 1)] = row[None]

    def label_copy(k):
        return pltpu.make_async_remote_copy(
            src_ref=lab.at[me],
            dst_ref=lab.at[me],
            send_sem=lab_send.at[k],
            recv_sem=lab_recv.at[me],
            device_id=(lax.rem(me + k, n_sta), g),
            device_id_type=MESH,
        )

    for k in range(1, n_sta):
        label_copy(k).start()

    sub = lax.broadcasted_iota(jnp.int32, (n_sta * CAP, LANES), 0)
    slot = jnp.full((n_sta * CAP, LANES), -1, jnp.int32)
    start = jnp.int32(0)
    for o in range(n_sta):
        held = count_ref[o]
        for k in range(CAP):
            chosen = order_ref[jnp.clip(start + k, 0, order_ref.shape[0] - 1)]
            slot = jnp.where(sub == o * CAP + k, jnp.where(k < held, chosen, -1), slot)
        start = start + held
    slots[...] = slot

    wide[...] = jnp.zeros_like(wide)
    for k in range(1, n_sta):
        src = lax.rem(me - k + n_sta, n_sta)
        pltpu.make_async_remote_copy(
            src_ref=lab.at[src], dst_ref=lab.at[src], send_sem=lab_send.at[k],
            recv_sem=lab_recv.at[src], device_id=(src, g), device_id_type=MESH,
        ).wait_recv()

    for c in range(1, chunks):
        for k in turns:
            for part in range(2):
                spectra_copy(c - 1, k, part).wait_send()
                spectra_copy(c, k, part).start()

    def widen(c, p):
        for part in range(2):
            for j in range(stations):
                wide[p, part, pl.ds(j, windows, stride=ROWS), :] = recv[c, p, part, j].astype(jnp.float32)

    def arrive(c, k):
        src = lax.rem(me - k + n_sta, n_sta)
        for part in range(2):
            pltpu.make_async_remote_copy(
                src_ref=recv.at[c, src, part], dst_ref=recv.at[c, src, part],
                send_sem=send_sem.at[c, k, part], recv_sem=recv_sem.at[c, src, part],
                device_id=(src, g), device_id_type=MESH,
            ).wait_recv()
        widen(c, src)

    def step(p, at_buffer):
        blocks = [lax.rem(p + r, n_sta) for r in range(rounds)]
        re = [[None] * stations for _ in range(rounds)]
        im = [[None] * stations for _ in range(rounds)]
        half = -(-stations // 2)
        for group in (range(half), range(half, stations)):
            for w in range(windows):
                at = pl.ds(w * ROWS, ROWS)
                mine = [(wide[b, 0, at, :], wide[b, 1, at, :]) for b in blocks]
                for j in group:
                    a = wide[p, 0, pl.ds(w * ROWS + j, ROWS, stride=0), :]
                    b = wide[p, 1, pl.ds(w * ROWS + j, ROWS, stride=0), :]
                    for r in range(rounds):
                        x, y = mine[r]
                        if w == 0:
                            re[r][j] = x * a + y * b
                            im[r][j] = y * a - x * b
                        else:
                            re[r][j] = re[r][j] + x * a + y * b
                            im[r][j] = im[r][j] + y * a - x * b
        blank = jnp.zeros((ROWS, LANES), jnp.float32)
        for r in range(rounds):
            at = pl.ds(r * ROWS * ROWS, ROWS * ROWS)
            pad = [blank] * (ROWS - stations)
            crossed[at_buffer, at, 0:LANES] = jnp.concatenate(re[r] + pad, axis=0).astype(jnp.bfloat16)
            crossed[at_buffer, at, LANES:] = jnp.concatenate(im[r] + pad, axis=0).astype(jnp.bfloat16)

    def binned(p, at_buffer):
        blocks = [lax.rem(p + r, n_sta) for r in range(rounds)]
        lanes = lax.broadcasted_iota(jnp.int32, (1, lab.shape[2]), 1)
        names = jnp.full((1, lab.shape[2]), -2, jnp.int32)
        for r in range(rounds):
            names = jnp.where(lanes // (ROWS * ROWS) == r, lab[blocks[r]], names)
        match = jnp.concatenate(
            [slots[...] == names[:, at:at + LANES] for at in range(0, lab.shape[2], LANES)], axis=1
        )
        match = jnp.where(match, 1.0, 0.0).astype(jnp.bfloat16)
        return jnp.dot(match, crossed[at_buffer], preferred_element_type=jnp.float32)

    def box_copies(c, o, part):
        q = part * halves + me // per_out
        t = lax.rem(me, per_out)
        col = pl.multiple_of(t * share + c * LANES, LANES)
        src = outbox.at[c, part, o]
        dst = inbox.at[g, :, pl.ds(col, LANES)]

        def far():
            return pltpu.make_async_remote_copy(
                src_ref=src, dst_ref=dst, send_sem=box_send.at[c, part, o],
                recv_sem=box_recv.at[c, t, g], device_id=(o, q), device_id_type=MESH,
            )

        def near():
            return pltpu.make_async_copy(src, dst, box_recv.at[c, t, g])

        return far, near, jnp.logical_and(o == me, q == g)

    def one_chunk(c, carry):
        for part in range(2):
            own_copy(c, part).wait()
        widen(c, me)
        arrive(c, 1)
        total[...] = jnp.zeros_like(total)
        crossed[...] = jnp.zeros_like(crossed)

        def one_step(k, carry):
            @pl.when(k < n_sta)
            def _():
                arrive(c, k)

            now = lax.rem(k, 2)
            total[...] += binned(lax.rem(me - k + 1 + 2 * n_sta, n_sta), 1 - now)
            step(lax.rem(me - k + 2 * n_sta, n_sta), now)
            return carry

        last = n_sta + rounds - 1
        lax.fori_loop(rounds - 1, last, one_step, 0)
        total[...] += binned(lax.rem(me - last + 1 + 2 * n_sta, n_sta), (last - 1) % 2)
        for part in range(2):
            for o in range(n_sta):
                outbox[c, part, o] = total[o * CAP:(o + 1) * CAP, part * LANES:(part + 1) * LANES]
        for part in range(2):
            for o in range(n_sta):
                far, near, is_me = box_copies(c, o, part)
                pl.when(is_me)(lambda near=near: near().start())
                pl.when(jnp.logical_not(is_me))(lambda far=far: far().start())
        return carry

    lax.fori_loop(0, chunks, one_chunk, 0)

    for c in range(chunks):
        for t in range(per_out):
            for s in range(n_win):
                dst = inbox.at[s, :, pl.ds(t * share + c * LANES, LANES)]
                pltpu.make_async_copy(dst, dst, box_recv.at[c, t, s]).wait()
    out_ref[...] = functools.reduce(jnp.add, [inbox[s] for s in range(n_win)])

    for k in turns:
        for part in range(2):
            spectra_copy(chunks - 1, k, part).wait_send()
    for c in range(chunks):
        for part in range(2):
            for o in range(n_sta):
                far, near, is_me = box_copies(c, o, part)
                pl.when(jnp.logical_not(is_me))(lambda far=far: far().wait_send())
    for k in range(1, n_sta):
        label_copy(k).wait_send()


def by_frequency(spectra, pair_bins, owner_count, bin_order):
    n_sta, n_win = lax.axis_size("sta"), lax.axis_size("win")
    windows, stations, columns = spectra.shape
    rounds = pair_bins.shape[1]
    width = columns // 2
    share = width // n_sta
    chunks = share // LANES
    out_cols = columns // n_win
    per_out = out_cols // share
    depth = -(-rounds * ROWS * ROWS // LANES) * LANES
    sizes = (n_sta, n_win, chunks, windows, stations, rounds, width)
    dma = pltpu.SemaphoreType.DMA
    sums = pl.pallas_call(
        functools.partial(kernel, sizes),
        out_shape=jax.ShapeDtypeStruct((CAP, out_cols), jnp.float32),
        in_specs=[
            pl.BlockSpec(memory_space=pl.ANY),
            pl.BlockSpec(memory_space=pltpu.SMEM),
            pl.BlockSpec(memory_space=pltpu.SMEM),
            pl.BlockSpec(memory_space=pltpu.SMEM),
        ],
        out_specs=pl.BlockSpec(memory_space=pltpu.VMEM),
        scratch_shapes=[
            pltpu.VMEM((chunks, n_sta, 2, stations, windows, LANES), spectra.dtype),
            pltpu.VMEM((n_sta, 2, windows * ROWS, LANES), jnp.float32),
            pltpu.VMEM((n_sta, 1, depth), jnp.int32),
            pltpu.VMEM((n_sta * CAP, LANES), jnp.int32),
            pltpu.VMEM((2, depth, 2 * LANES), jnp.bfloat16),
            pltpu.VMEM((n_sta * CAP, 2 * LANES), jnp.float32),
            pltpu.VMEM((chunks, 2, n_sta, CAP, LANES), jnp.float32),
            pltpu.VMEM((n_win, CAP, out_cols), jnp.float32),
            dma((chunks, n_sta, 2)),
            dma((chunks, n_sta, 2)),
            dma((chunks, 2)),
            dma((n_sta,)),
            dma((n_sta,)),
            dma((chunks, 2, n_sta)),
            dma((chunks, per_out, n_win)),
        ],
        compiler_params=pltpu.CompilerParams(
            collective_id=0, has_side_effects=True, vmem_limit_bytes=56 * 1024 * 1024
        ),
        cost_estimate=pl.CostEstimate(
            flops=8 * width * windows * rounds * stations * stations,
            bytes_accessed=2 * spectra.size, transcendentals=0,
        ),
    )(jnp.transpose(spectra, (1, 0, 2)), jnp.transpose(pair_bins, (1, 0, 2)), owner_count, bin_order)
    return sums * jnp.float32(1.0 / (windows * n_win))


def on_device(spectra, pair_bins, owner_count, bin_order):
    n_sta, n_win = lax.axis_size("sta"), lax.axis_size("win")
    width = spectra.shape[2] // 2
    share, out_cols = width // n_sta, 2 * width // n_win
    fits = (
        width % (n_sta * LANES) == 0 and out_cols % share == 0 and width % out_cols == 0
        and spectra.shape[1] <= ROWS and pair_bins.shape[1] <= n_sta - 1
    )
    plan = by_frequency if fits else by_blocks
    return plan(spectra, pair_bins, owner_count, bin_order)


def solution(mesh):
    return jax.shard_map(
        on_device,
        mesh=mesh,
        in_specs=(P("win", "sta", None), P("sta", None, None), P(), P()),
        out_specs=P("sta", "win"),
        check_vma=False,
    )
```

```python
import functools
import jax
import jax.numpy as jnp
from jax import lax
from jax.experimental import pallas as pl
from jax.experimental.pallas import tpu as pltpu
from jax.sharding import PartitionSpec as P

CAP = 4
LANES = 128
ROWS = 8
MESH = pl.DeviceIdType.MESH


def passed_along(value, axis, steps):
    count = lax.axis_size(axis)
    pairs = [(source, (source + steps) % count) for source in range(count)]
    return lax.ppermute(value, axis, pairs)


def cross_pairs(own, other):
    width = own.shape[-1] // 2
    own_re, own_im = (own[..., :width], own[..., width:])
    other_re, other_im = (other[..., :width], other[..., width:])
    form = "wsf,wtf->stf"
    real = jnp.einsum(form, own_re, other_re, preferred_element_type=jnp.float32) + jnp.einsum(
        form, own_im, other_im, preferred_element_type=jnp.float32
    )
    imag = jnp.einsum(form, own_im, other_re, preferred_element_type=jnp.float32) - jnp.einsum(
        form, own_re, other_im, preferred_element_type=jnp.float32
    )
    joined = jnp.concatenate([real, imag], axis=-1).astype(jnp.bfloat16)
    return joined.reshape(-1, joined.shape[-1])


def by_blocks(spectra, pair_bins, owner_count, bin_order):
    rounds = pair_bins.shape[1]
    blocks = [spectra]
    for offset in range(1, rounds):
        blocks.append(passed_along(spectra, "sta", offset))
    crossed = jnp.concatenate([cross_pairs(spectra, other) for other in blocks], axis=0)
    labels = jnp.transpose(pair_bins, (1, 0, 2)).reshape(-1)
    bin_total = bin_order.shape[0]
    starts = jnp.cumsum(owner_count) - owner_count
    ranks = jnp.arange(CAP, dtype=jnp.int32)
    positions = jnp.clip(starts[:, None] + ranks[None, :], 0, bin_total - 1)
    valid = ranks[None, :] < owner_count[:, None]
    chosen = jnp.take(bin_order, positions)
    slot_bin = jnp.where(valid, chosen, -1).reshape(-1)
    window_total = spectra.shape[0] * lax.axis_size("win")
    matches = (slot_bin[:, None] == labels[None, :]).astype(jnp.bfloat16)
    partial_sums = jnp.dot(matches, crossed, preferred_element_type=jnp.float32)
    spread = lax.psum_scatter(partial_sums, "win", scatter_dimension=1, tiled=True)
    stacks = lax.psum_scatter(spread, "sta", scatter_dimension=0, tiled=True)
    return stacks * jnp.float32(1.0 / window_total)


def kernel(
    sizes, spec_ref, bins_ref, count_ref, order_ref, out_ref,
    recv, wide, lab, slots, crossed, total, outbox, inbox,
    send_sem, recv_sem, own_sem, lab_send, lab_recv, box_send, box_recv,
):
    n_sta, n_win, chunks, windows, stations, rounds, width = sizes
    share = width // n_sta
    out_cols = out_ref.shape[1]
    per_out = out_cols // share
    halves = width // out_cols
    me = lax.axis_index("sta")
    g = lax.axis_index("win")

    barrier = pltpu.get_barrier_semaphore()
    for t in range(1, n_sta):
        pl.semaphore_signal(
            barrier, inc=1, device_id=(lax.rem(me + t, n_sta), g), device_id_type=MESH
        )
    for t in range(1, n_win):
        pl.semaphore_signal(
            barrier, inc=1, device_id=(me, lax.rem(g + t, n_win)), device_id_type=MESH
        )
    pl.semaphore_wait(barrier, n_sta + n_win - 2)

    def partner(k):
        if n_sta & (n_sta - 1):
            return lax.rem(me + k, n_sta)
        digits, bit = me, 1
        while bit < n_sta:
            if k & bit:
                digits = digits + bit - 2 * bit * lax.rem(digits // bit, 2)
            bit *= 2
        return digits

    far_half = list(range(n_sta // 2, n_sta))
    near_half = list(range(1, n_sta // 2)) + [None]
    turns = [k for pair in zip(far_half, near_half) for k in pair if k is not None]

    def share_of(dest, c, part):
        col = pl.multiple_of(part * width + dest * share + c * LANES, LANES)
        return spec_ref.at[:, :, pl.ds(col, LANES)]

    def spectra_copy(c, k, part):
        dest = partner(k)
        return pltpu.make_async_remote_copy(
            src_ref=share_of(dest, c, part),
            dst_ref=recv.at[c, me, part],
            send_sem=send_sem.at[c, k, part],
            recv_sem=recv_sem.at[c, me, part],
            device_id=(dest, g),
            device_id_type=MESH,
        )

    def own_copy(c, part):
        return pltpu.make_async_copy(share_of(me, c, part), recv.at[c, me, part], own_sem.at[c, part])

    for c in range(chunks):
        for part in range(2):
            own_copy(c, part).start()
    for k in turns:
        for part in range(2):
            spectra_copy(0, k, part).start()

    lane = lax.broadcasted_iota(jnp.int32, (1, lab.shape[2]), 1)
    row = jnp.full((1, lab.shape[2]), -2, jnp.int32)
    for r in range(rounds):
        for j in range(stations):
            for i in range(stations):
                row = jnp.where(lane == (r * ROWS + j) * ROWS + i, bins_ref[r, i, j], row)
    lab[pl.ds(me, 1)] = row[None]

    def label_copy(k):
        return pltpu.make_async_remote_copy(
            src_ref=lab.at[me],
            dst_ref=lab.at[me],
            send_sem=lab_send.at[k],
            recv_sem=lab_recv.at[me],
            device_id=(lax.rem(me + k, n_sta), g),
            device_id_type=MESH,
        )

    for k in range(1, n_sta):
        label_copy(k).start()

    sub = lax.broadcasted_iota(jnp.int32, (n_sta * CAP, LANES), 0)
    slot = jnp.full((n_sta * CAP, LANES), -1, jnp.int32)
    start = jnp.int32(0)
    for o in range(n_sta):
        held = count_ref[o]
        for k in range(CAP):
            chosen = order_ref[jnp.clip(start + k, 0, order_ref.shape[0] - 1)]
            slot = jnp.where(sub == o * CAP + k, jnp.where(k < held, chosen, -1), slot)
        start = start + held
    slots[...] = slot

    wide[...] = jnp.zeros_like(wide)
    for k in range(1, n_sta):
        src = lax.rem(me - k + n_sta, n_sta)
        pltpu.make_async_remote_copy(
            src_ref=lab.at[src], dst_ref=lab.at[src], send_sem=lab_send.at[k],
            recv_sem=lab_recv.at[src], device_id=(src, g), device_id_type=MESH,
        ).wait_recv()

    for c in range(1, chunks):
        for k in turns:
            for part in range(2):
                spectra_copy(c - 1, k, part).wait_send()
                spectra_copy(c, k, part).start()

    def widen(c, p):
        for part in range(2):
            for j in range(stations):
                wide[p, part, pl.ds(j, windows, stride=ROWS), :] = recv[c, p, part, j].astype(jnp.float32)

    def arrive(c, k):
        src = lax.rem(me - k + n_sta, n_sta)
        for part in range(2):
            pltpu.make_async_remote_copy(
                src_ref=recv.at[c, src, part], dst_ref=recv.at[c, src, part],
                send_sem=send_sem.at[c, k, part], recv_sem=recv_sem.at[c, src, part],
                device_id=(src, g), device_id_type=MESH,
            ).wait_recv()
        widen(c, src)

    def step(p, at_buffer):
        blocks = [lax.rem(p + r, n_sta) for r in range(rounds)]
        re = [[None] * stations for _ in range(rounds)]
        im = [[None] * stations for _ in range(rounds)]
        half = -(-stations // 2)
        for group in (range(half), range(half, stations)):
            for w in range(windows):
                at = pl.ds(w * ROWS, ROWS)
                mine = [(wide[b, 0, at, :], wide[b, 1, at, :]) for b in blocks]
                for j in group:
                    a = wide[p, 0, pl.ds(w * ROWS + j, ROWS, stride=0), :]
                    b = wide[p, 1, pl.ds(w * ROWS + j, ROWS, stride=0), :]
                    for r in range(rounds):
                        x, y = mine[r]
                        if w == 0:
                            re[r][j] = x * a + y * b
                            im[r][j] = y * a - x * b
                        else:
                            re[r][j] = re[r][j] + x * a + y * b
                            im[r][j] = im[r][j] + y * a - x * b
        blank = jnp.zeros((ROWS, LANES), jnp.float32)
        for r in range(rounds):
            at = pl.ds(r * ROWS * ROWS, ROWS * ROWS)
            pad = [blank] * (ROWS - stations)
            crossed[at_buffer, at, 0:LANES] = jnp.concatenate(re[r] + pad, axis=0).astype(jnp.bfloat16)
            crossed[at_buffer, at, LANES:] = jnp.concatenate(im[r] + pad, axis=0).astype(jnp.bfloat16)

    def binned(p, at_buffer):
        blocks = [lax.rem(p + r, n_sta) for r in range(rounds)]
        lanes = lax.broadcasted_iota(jnp.int32, (1, lab.shape[2]), 1)
        names = jnp.full((1, lab.shape[2]), -2, jnp.int32)
        for r in range(rounds):
            names = jnp.where(lanes // (ROWS * ROWS) == r, lab[blocks[r]], names)
        match = jnp.concatenate(
            [slots[...] == names[:, at:at + LANES] for at in range(0, lab.shape[2], LANES)], axis=1
        )
        match = jnp.where(match, 1.0, 0.0).astype(jnp.bfloat16)
        return jnp.dot(match, crossed[at_buffer], preferred_element_type=jnp.float32)

    def box_copies(c, o, part):
        q = part * halves + me // per_out
        t = lax.rem(me, per_out)
        col = pl.multiple_of(t * share + c * LANES, LANES)
        src = outbox.at[c, part, o]
        dst = inbox.at[g, :, pl.ds(col, LANES)]

        def far():
            return pltpu.make_async_remote_copy(
                src_ref=src, dst_ref=dst, send_sem=box_send.at[c, part, o],
                recv_sem=box_recv.at[c, t, g], device_id=(o, q), device_id_type=MESH,
            )

        def near():
            return pltpu.make_async_copy(src, dst, box_recv.at[c, t, g])

        return far, near, jnp.logical_and(o == me, q == g)

    def one_chunk(c, carry):
        for part in range(2):
            own_copy(c, part).wait()
        widen(c, me)
        arrive(c, 1)
        total[...] = jnp.zeros_like(total)
        crossed[...] = jnp.zeros_like(crossed)

        def one_step(k, carry):
            @pl.when(k < n_sta)
            def _():
                arrive(c, k)

            now = lax.rem(k, 2)
            total[...] += binned(lax.rem(me - k + 1 + 2 * n_sta, n_sta), 1 - now)
            step(lax.rem(me - k + 2 * n_sta, n_sta), now)
            return carry

        last = n_sta + rounds - 1
        lax.fori_loop(rounds - 1, last, one_step, 0)
        total[...] += binned(lax.rem(me - last + 1 + 2 * n_sta, n_sta), (last - 1) % 2)
        for part in range(2):
            for o in range(n_sta):
                outbox[c, part, o] = total[o * CAP:(o + 1) * CAP, part * LANES:(part + 1) * LANES]
        for part in range(2):
            for o in range(n_sta):
                far, near, is_me = box_copies(c, o, part)
                pl.when(is_me)(lambda near=near: near().start())
                pl.when(jnp.logical_not(is_me))(lambda far=far: far().start())
        return carry

    lax.fori_loop(0, chunks, one_chunk, 0)

    for c in range(chunks):
        for t in range(per_out):
            for s in range(n_win):
                dst = inbox.at[s, :, pl.ds(t * share + c * LANES, LANES)]
                pltpu.make_async_copy(dst, dst, box_recv.at[c, t, s]).wait()
    out_ref[...] = functools.reduce(jnp.add, [inbox[s] for s in range(n_win)])

    for k in turns:
        for part in range(2):
            spectra_copy(chunks - 1, k, part).wait_send()
    for c in range(chunks):
        for part in range(2):
            for o in range(n_sta):
                far, near, is_me = box_copies(c, o, part)
                pl.when(jnp.logical_not(is_me))(lambda far=far: far().wait_send())
    for k in range(1, n_sta):
        label_copy(k).wait_send()


def by_frequency(spectra, pair_bins, owner_count, bin_order):
    n_sta, n_win = lax.axis_size("sta"), lax.axis_size("win")
    windows, stations, columns = spectra.shape
    rounds = pair_bins.shape[1]
    width = columns // 2
    share = width // n_sta
    chunks = share // LANES
    out_cols = columns // n_win
    per_out = out_cols // share
    depth = -(-rounds * ROWS * ROWS // LANES) * LANES
    sizes = (n_sta, n_win, chunks, windows, stations, rounds, width)
    dma = pltpu.SemaphoreType.DMA
    sums = pl.pallas_call(
        functools.partial(kernel, sizes),
        out_shape=jax.ShapeDtypeStruct((CAP, out_cols), jnp.float32),
        in_specs=[
            pl.BlockSpec(memory_space=pltpu.VMEM),
            pl.BlockSpec(memory_space=pltpu.SMEM),
            pl.BlockSpec(memory_space=pltpu.SMEM),
            pl.BlockSpec(memory_space=pltpu.SMEM),
        ],
        out_specs=pl.BlockSpec(memory_space=pltpu.VMEM),
        scratch_shapes=[
            pltpu.VMEM((chunks, n_sta, 2, stations, windows, LANES), spectra.dtype),
            pltpu.VMEM((n_sta, 2, windows * ROWS, LANES), jnp.float32),
            pltpu.VMEM((n_sta, 1, depth), jnp.int32),
            pltpu.VMEM((n_sta * CAP, LANES), jnp.int32),
            pltpu.VMEM((2, depth, 2 * LANES), jnp.bfloat16),
            pltpu.VMEM((n_sta * CAP, 2 * LANES), jnp.float32),
            pltpu.VMEM((chunks, 2, n_sta, CAP, LANES), jnp.float32),
            pltpu.VMEM((n_win, CAP, out_cols), jnp.float32),
            dma((chunks, n_sta, 2)),
            dma((chunks, n_sta, 2)),
            dma((chunks, 2)),
            dma((n_sta,)),
            dma((n_sta,)),
            dma((chunks, 2, n_sta)),
            dma((chunks, per_out, n_win)),
        ],
        compiler_params=pltpu.CompilerParams(
            collective_id=0, has_side_effects=True, vmem_limit_bytes=56 * 1024 * 1024
        ),
        cost_estimate=pl.CostEstimate(
            flops=8 * width * windows * rounds * stations * stations,
            bytes_accessed=2 * spectra.size, transcendentals=0,
        ),
    )(jnp.transpose(spectra, (1, 0, 2)), jnp.transpose(pair_bins, (1, 0, 2)), owner_count, bin_order)
    return sums * jnp.float32(1.0 / (windows * n_win))


def on_device(spectra, pair_bins, owner_count, bin_order):
    n_sta, n_win = lax.axis_size("sta"), lax.axis_size("win")
    width = spectra.shape[2] // 2
    share, out_cols = width // n_sta, 2 * width // n_win
    fits = (
        width % (n_sta * LANES) == 0 and out_cols % share == 0 and width % out_cols == 0
        and spectra.shape[1] <= ROWS and pair_bins.shape[1] <= n_sta - 1
    )
    plan = by_frequency if fits else by_blocks
    return plan(spectra, pair_bins, owner_count, bin_order)


def solution(mesh):
    return jax.shard_map(
        on_device,
        mesh=mesh,
        in_specs=(P("win", "sta", None), P("sta", None, None), P(), P()),
        out_specs=P("sta", "win"),
        check_vma=False,
    )
```

```python
import functools
import jax
import jax.numpy as jnp
from jax import lax
from jax.experimental import pallas as pl
from jax.experimental.pallas import tpu as pltpu
from jax.sharding import PartitionSpec as P

CAP = 4
LANES = 128
ROWS = 8
MESH = pl.DeviceIdType.MESH


def passed_along(value, axis, steps):
    count = lax.axis_size(axis)
    pairs = [(source, (source + steps) % count) for source in range(count)]
    return lax.ppermute(value, axis, pairs)


def cross_pairs(own, other):
    width = own.shape[-1] // 2
    own_re, own_im = (own[..., :width], own[..., width:])
    other_re, other_im = (other[..., :width], other[..., width:])
    form = "wsf,wtf->stf"
    real = jnp.einsum(form, own_re, other_re, preferred_element_type=jnp.float32) + jnp.einsum(
        form, own_im, other_im, preferred_element_type=jnp.float32
    )
    imag = jnp.einsum(form, own_im, other_re, preferred_element_type=jnp.float32) - jnp.einsum(
        form, own_re, other_im, preferred_element_type=jnp.float32
    )
    joined = jnp.concatenate([real, imag], axis=-1).astype(jnp.bfloat16)
    return joined.reshape(-1, joined.shape[-1])


def by_blocks(spectra, pair_bins, owner_count, bin_order):
    rounds = pair_bins.shape[1]
    blocks = [spectra]
    for offset in range(1, rounds):
        blocks.append(passed_along(spectra, "sta", offset))
    crossed = jnp.concatenate([cross_pairs(spectra, other) for other in blocks], axis=0)
    labels = jnp.transpose(pair_bins, (1, 0, 2)).reshape(-1)
    bin_total = bin_order.shape[0]
    starts = jnp.cumsum(owner_count) - owner_count
    ranks = jnp.arange(CAP, dtype=jnp.int32)
    positions = jnp.clip(starts[:, None] + ranks[None, :], 0, bin_total - 1)
    valid = ranks[None, :] < owner_count[:, None]
    chosen = jnp.take(bin_order, positions)
    slot_bin = jnp.where(valid, chosen, -1).reshape(-1)
    window_total = spectra.shape[0] * lax.axis_size("win")
    matches = (slot_bin[:, None] == labels[None, :]).astype(jnp.bfloat16)
    partial_sums = jnp.dot(matches, crossed, preferred_element_type=jnp.float32)
    spread = lax.psum_scatter(partial_sums, "win", scatter_dimension=1, tiled=True)
    stacks = lax.psum_scatter(spread, "sta", scatter_dimension=0, tiled=True)
    return stacks * jnp.float32(1.0 / window_total)


def kernel(
    sizes, spec_ref, bins_ref, count_ref, order_ref, out_ref,
    stage, recv, wide, lab, slots, crossed, total, outbox, inbox,
    stage_sem, send_sem, recv_sem, own_sem, lab_send, lab_recv, box_send, box_recv,
):
    n_sta, n_win, chunks, windows, stations, rounds, width = sizes
    share = width // n_sta
    out_cols = out_ref.shape[1]
    per_out = out_cols // share
    halves = width // out_cols
    me = lax.axis_index("sta")
    g = lax.axis_index("win")

    def partner(k):
        if n_sta & (n_sta - 1):
            return lax.rem(me + k, n_sta)
        digits, bit = me, 1
        while bit < n_sta:
            if k & bit:
                digits = digits + bit - 2 * bit * lax.rem(digits // bit, 2)
            bit *= 2
        return digits

    far_half = list(range(n_sta // 2, n_sta))
    near_half = list(range(1, n_sta // 2)) + [None]
    turns = [k for pair in zip(far_half, near_half) for k in pair if k is not None]

    def share_of(dest, c, part):
        col = pl.multiple_of(part * width + dest * share + c * LANES, LANES)
        return spec_ref.at[:, :, pl.ds(col, LANES)]

    def stage_copy(c, k, part):
        return pltpu.make_async_copy(share_of(partner(k), c, part), stage.at[c, k, part], stage_sem.at[c, k, part])

    def own_copy(c, part):
        return pltpu.make_async_copy(share_of(me, c, part), recv.at[c, me, part], own_sem.at[c, part])

    def spectra_copy(c, k):
        return pltpu.make_async_remote_copy(
            src_ref=stage.at[c, k],
            dst_ref=recv.at[c, me],
            send_sem=send_sem.at[c, k],
            recv_sem=recv_sem.at[c, me],
            device_id=(partner(k), g),
            device_id_type=MESH,
        )

    for c in range(chunks):
        for k in turns:
            for part in range(2):
                stage_copy(c, k, part).start()
        for part in range(2):
            own_copy(c, part).start()

    barrier = pltpu.get_barrier_semaphore()
    for t in range(1, n_sta):
        pl.semaphore_signal(
            barrier, inc=1, device_id=(lax.rem(me + t, n_sta), g), device_id_type=MESH
        )
    for t in range(1, n_win):
        pl.semaphore_signal(
            barrier, inc=1, device_id=(me, lax.rem(g + t, n_win)), device_id_type=MESH
        )
    pl.semaphore_wait(barrier, n_sta + n_win - 2)

    for k in turns:
        for part in range(2):
            stage_copy(0, k, part).wait()
        spectra_copy(0, k).start()

    lane = lax.broadcasted_iota(jnp.int32, (1, lab.shape[2]), 1)
    row = jnp.full((1, lab.shape[2]), -2, jnp.int32)
    for r in range(rounds):
        for j in range(stations):
            for i in range(stations):
                row = jnp.where(lane == (r * ROWS + j) * ROWS + i, bins_ref[r, i, j], row)
    lab[pl.ds(me, 1)] = row[None]

    def label_copy(k):
        return pltpu.make_async_remote_copy(
            src_ref=lab.at[me],
            dst_ref=lab.at[me],
            send_sem=lab_send.at[k],
            recv_sem=lab_recv.at[me],
            device_id=(lax.rem(me + k, n_sta), g),
            device_id_type=MESH,
        )

    for k in range(1, n_sta):
        label_copy(k).start()

    sub = lax.broadcasted_iota(jnp.int32, (n_sta * CAP, LANES), 0)
    slot = jnp.full((n_sta * CAP, LANES), -1, jnp.int32)
    start = jnp.int32(0)
    for o in range(n_sta):
        held = count_ref[o]
        for k in range(CAP):
            chosen = order_ref[jnp.clip(start + k, 0, order_ref.shape[0] - 1)]
            slot = jnp.where(sub == o * CAP + k, jnp.where(k < held, chosen, -1), slot)
        start = start + held
    slots[...] = slot

    wide[...] = jnp.zeros_like(wide)
    for k in range(1, n_sta):
        src = lax.rem(me - k + n_sta, n_sta)
        pltpu.make_async_remote_copy(
            src_ref=lab.at[src], dst_ref=lab.at[src], send_sem=lab_send.at[k],
            recv_sem=lab_recv.at[src], device_id=(src, g), device_id_type=MESH,
        ).wait_recv()

    for c in range(1, chunks):
        for k in turns:
            for part in range(2):
                stage_copy(c, k, part).wait()
            spectra_copy(c - 1, k).wait_send()
            spectra_copy(c, k).start()

    def widen(c, p):
        for part in range(2):
            for j in range(stations):
                wide[p, part, pl.ds(j, windows, stride=ROWS), :] = recv[c, p, part, j].astype(jnp.float32)

    def arrive(c, k):
        src = lax.rem(me - k + n_sta, n_sta)
        pltpu.make_async_remote_copy(
            src_ref=recv.at[c, src], dst_ref=recv.at[c, src],
            send_sem=send_sem.at[c, k], recv_sem=recv_sem.at[c, src],
            device_id=(src, g), device_id_type=MESH,
        ).wait_recv()
        widen(c, src)

    def step(p, at_buffer):
        blocks = [lax.rem(p + r, n_sta) for r in range(rounds)]
        re = [[None] * stations for _ in range(rounds)]
        im = [[None] * stations for _ in range(rounds)]
        half = -(-stations // 2)
        for group in (range(half), range(half, stations)):
            for w in range(windows):
                at = pl.ds(w * ROWS, ROWS)
                mine = [(wide[b, 0, at, :], wide[b, 1, at, :]) for b in blocks]
                for j in group:
                    a = wide[p, 0, pl.ds(w * ROWS + j, ROWS, stride=0), :]
                    b = wide[p, 1, pl.ds(w * ROWS + j, ROWS, stride=0), :]
                    for r in range(rounds):
                        x, y = mine[r]
                        if w == 0:
                            re[r][j] = x * a + y * b
                            im[r][j] = y * a - x * b
                        else:
                            re[r][j] = re[r][j] + x * a + y * b
                            im[r][j] = im[r][j] + y * a - x * b
        blank = jnp.zeros((ROWS, LANES), jnp.float32)
        for r in range(rounds):
            at = pl.ds(r * ROWS * ROWS, ROWS * ROWS)
            pad = [blank] * (ROWS - stations)
            crossed[at_buffer, at, 0:LANES] = jnp.concatenate(re[r] + pad, axis=0).astype(jnp.bfloat16)
            crossed[at_buffer, at, LANES:] = jnp.concatenate(im[r] + pad, axis=0).astype(jnp.bfloat16)

    def binned(p, at_buffer):
        blocks = [lax.rem(p + r, n_sta) for r in range(rounds)]
        lanes = lax.broadcasted_iota(jnp.int32, (1, lab.shape[2]), 1)
        names = jnp.full((1, lab.shape[2]), -2, jnp.int32)
        for r in range(rounds):
            names = jnp.where(lanes // (ROWS * ROWS) == r, lab[blocks[r]], names)
        match = jnp.concatenate(
            [slots[...] == names[:, at:at + LANES] for at in range(0, lab.shape[2], LANES)], axis=1
        )
        match = jnp.where(match, 1.0, 0.0).astype(jnp.bfloat16)
        return jnp.dot(match, crossed[at_buffer], preferred_element_type=jnp.float32)

    def box_copies(c, o, part):
        q = part * halves + me // per_out
        t = lax.rem(me, per_out)
        col = pl.multiple_of(t * share + c * LANES, LANES)
        src = outbox.at[c, part, o]
        dst = inbox.at[g, :, pl.ds(col, LANES)]

        def far():
            return pltpu.make_async_remote_copy(
                src_ref=src, dst_ref=dst, send_sem=box_send.at[c, part, o],
                recv_sem=box_recv.at[c, t, g], device_id=(o, q), device_id_type=MESH,
            )

        def near():
            return pltpu.make_async_copy(src, dst, box_recv.at[c, t, g])

        return far, near, jnp.logical_and(o == me, q == g)

    def one_chunk(c, carry):
        for part in range(2):
            own_copy(c, part).wait()
        widen(c, me)
        arrive(c, 1)
        total[...] = jnp.zeros_like(total)
        crossed[...] = jnp.zeros_like(crossed)

        def one_step(k, carry):
            @pl.when(k < n_sta)
            def _():
                arrive(c, k)

            now = lax.rem(k, 2)
            total[...] += binned(lax.rem(me - k + 1 + 2 * n_sta, n_sta), 1 - now)
            step(lax.rem(me - k + 2 * n_sta, n_sta), now)
            return carry

        last = n_sta + rounds - 1
        lax.fori_loop(rounds - 1, last, one_step, 0)
        total[...] += binned(lax.rem(me - last + 1 + 2 * n_sta, n_sta), (last - 1) % 2)
        for part in range(2):
            for o in range(n_sta):
                outbox[c, part, o] = total[o * CAP:(o + 1) * CAP, part * LANES:(part + 1) * LANES]
        for part in range(2):
            for o in range(n_sta):
                far, near, is_me = box_copies(c, o, part)
                pl.when(is_me)(lambda near=near: near().start())
                pl.when(jnp.logical_not(is_me))(lambda far=far: far().start())
        return carry

    lax.fori_loop(0, chunks, one_chunk, 0)

    for c in range(chunks):
        for t in range(per_out):
            for s in range(n_win):
                dst = inbox.at[s, :, pl.ds(t * share + c * LANES, LANES)]
                pltpu.make_async_copy(dst, dst, box_recv.at[c, t, s]).wait()
    out_ref[...] = functools.reduce(jnp.add, [inbox[s] for s in range(n_win)])

    for k in turns:
        spectra_copy(chunks - 1, k).wait_send()
    for c in range(chunks):
        for part in range(2):
            for o in range(n_sta):
                far, near, is_me = box_copies(c, o, part)
                pl.when(jnp.logical_not(is_me))(lambda far=far: far().wait_send())
    for k in range(1, n_sta):
        label_copy(k).wait_send()


def by_frequency(spectra, pair_bins, owner_count, bin_order):
    n_sta, n_win = lax.axis_size("sta"), lax.axis_size("win")
    windows, stations, columns = spectra.shape
    rounds = pair_bins.shape[1]
    width = columns // 2
    share = width // n_sta
    chunks = share // LANES
    out_cols = columns // n_win
    per_out = out_cols // share
    depth = -(-rounds * ROWS * ROWS // LANES) * LANES
    sizes = (n_sta, n_win, chunks, windows, stations, rounds, width)
    dma = pltpu.SemaphoreType.DMA
    sums = pl.pallas_call(
        functools.partial(kernel, sizes),
        out_shape=jax.ShapeDtypeStruct((CAP, out_cols), jnp.float32),
        in_specs=[
            pl.BlockSpec(memory_space=pl.ANY),
            pl.BlockSpec(memory_space=pltpu.SMEM),
            pl.BlockSpec(memory_space=pltpu.SMEM),
            pl.BlockSpec(memory_space=pltpu.SMEM),
        ],
        out_specs=pl.BlockSpec(memory_space=pltpu.VMEM),
        scratch_shapes=[
            pltpu.VMEM((chunks, n_sta, 2, stations, windows, LANES), spectra.dtype),
            pltpu.VMEM((chunks, n_sta, 2, stations, windows, LANES), spectra.dtype),
            pltpu.VMEM((n_sta, 2, windows * ROWS, LANES), jnp.float32),
            pltpu.VMEM((n_sta, 1, depth), jnp.int32),
            pltpu.VMEM((n_sta * CAP, LANES), jnp.int32),
            pltpu.VMEM((2, depth, 2 * LANES), jnp.bfloat16),
            pltpu.VMEM((n_sta * CAP, 2 * LANES), jnp.float32),
            pltpu.VMEM((chunks, 2, n_sta, CAP, LANES), jnp.float32),
            pltpu.VMEM((n_win, CAP, out_cols), jnp.float32),
            dma((chunks, n_sta, 2)),
            dma((chunks, n_sta)),
            dma((chunks, n_sta)),
            dma((chunks, 2)),
            dma((n_sta,)),
            dma((n_sta,)),
            dma((chunks, 2, n_sta)),
            dma((chunks, per_out, n_win)),
        ],
        compiler_params=pltpu.CompilerParams(
            collective_id=0, has_side_effects=True, vmem_limit_bytes=56 * 1024 * 1024
        ),
        cost_estimate=pl.CostEstimate(
            flops=8 * width * windows * rounds * stations * stations,
            bytes_accessed=2 * spectra.size, transcendentals=0,
        ),
    )(jnp.transpose(spectra, (1, 0, 2)), jnp.transpose(pair_bins, (1, 0, 2)), owner_count, bin_order)
    return sums * jnp.float32(1.0 / (windows * n_win))


def on_device(spectra, pair_bins, owner_count, bin_order):
    n_sta, n_win = lax.axis_size("sta"), lax.axis_size("win")
    width = spectra.shape[2] // 2
    share, out_cols = width // n_sta, 2 * width // n_win
    fits = (
        width % (n_sta * LANES) == 0 and out_cols % share == 0 and width % out_cols == 0
        and spectra.shape[1] <= ROWS and pair_bins.shape[1] <= n_sta - 1
    )
    plan = by_frequency if fits else by_blocks
    return plan(spectra, pair_bins, owner_count, bin_order)


def solution(mesh):
    return jax.shard_map(
        on_device,
        mesh=mesh,
        in_specs=(P("win", "sta", None), P("sta", None, None), P(), P()),
        out_specs=P("sta", "win"),
        check_vma=False,
    )
```

```python
import functools
import jax
import jax.numpy as jnp
from jax import lax
from jax.experimental import pallas as pl
from jax.experimental.pallas import tpu as pltpu
from jax.sharding import PartitionSpec as P

CAP = 4
LANES = 128
ROWS = 8
MESH = pl.DeviceIdType.MESH


def passed_along(value, axis, steps):
    count = lax.axis_size(axis)
    pairs = [(source, (source + steps) % count) for source in range(count)]
    return lax.ppermute(value, axis, pairs)


def cross_pairs(own, other):
    width = own.shape[-1] // 2
    own_re, own_im = (own[..., :width], own[..., width:])
    other_re, other_im = (other[..., :width], other[..., width:])
    form = "wsf,wtf->stf"
    real = jnp.einsum(form, own_re, other_re, preferred_element_type=jnp.float32) + jnp.einsum(
        form, own_im, other_im, preferred_element_type=jnp.float32
    )
    imag = jnp.einsum(form, own_im, other_re, preferred_element_type=jnp.float32) - jnp.einsum(
        form, own_re, other_im, preferred_element_type=jnp.float32
    )
    joined = jnp.concatenate([real, imag], axis=-1).astype(jnp.bfloat16)
    return joined.reshape(-1, joined.shape[-1])


def by_blocks(spectra, pair_bins, owner_count, bin_order):
    rounds = pair_bins.shape[1]
    blocks = [spectra]
    for offset in range(1, rounds):
        blocks.append(passed_along(spectra, "sta", offset))
    crossed = jnp.concatenate([cross_pairs(spectra, other) for other in blocks], axis=0)
    labels = jnp.transpose(pair_bins, (1, 0, 2)).reshape(-1)
    bin_total = bin_order.shape[0]
    starts = jnp.cumsum(owner_count) - owner_count
    ranks = jnp.arange(CAP, dtype=jnp.int32)
    positions = jnp.clip(starts[:, None] + ranks[None, :], 0, bin_total - 1)
    valid = ranks[None, :] < owner_count[:, None]
    chosen = jnp.take(bin_order, positions)
    slot_bin = jnp.where(valid, chosen, -1).reshape(-1)
    window_total = spectra.shape[0] * lax.axis_size("win")
    matches = (slot_bin[:, None] == labels[None, :]).astype(jnp.bfloat16)
    partial_sums = jnp.dot(matches, crossed, preferred_element_type=jnp.float32)
    spread = lax.psum_scatter(partial_sums, "win", scatter_dimension=1, tiled=True)
    stacks = lax.psum_scatter(spread, "sta", scatter_dimension=0, tiled=True)
    return stacks * jnp.float32(1.0 / window_total)


def kernel(
    sizes, spec_ref, bins_ref, count_ref, order_ref, out_ref,
    stage, recv, wide, lab, slots, crossed, total, outbox, inbox,
    stage_sem, send_sem, recv_sem, own_sem, lab_send, lab_recv, box_send, box_recv,
):
    n_sta, n_win, chunks, windows, stations, rounds, width = sizes
    share = width // n_sta
    out_cols = out_ref.shape[1]
    per_out = out_cols // share
    halves = width // out_cols
    me = lax.axis_index("sta")
    g = lax.axis_index("win")

    def partner(k):
        if n_sta & (n_sta - 1):
            return lax.rem(me + k, n_sta)
        digits, bit = me, 1
        while bit < n_sta:
            if k & bit:
                digits = digits + bit - 2 * bit * lax.rem(digits // bit, 2)
            bit *= 2
        return digits

    far_half = list(range(n_sta // 2, n_sta))
    near_half = list(range(1, n_sta // 2)) + [None]
    turns = [k for pair in zip(far_half, near_half) for k in pair if k is not None]

    def share_of(dest, c, part):
        col = pl.multiple_of(part * width + dest * share + c * LANES, LANES)
        return spec_ref.at[:, :, pl.ds(col, LANES)]

    def stage_copy(c, k, part):
        return pltpu.make_async_copy(share_of(partner(k), c, part), stage.at[c, k, part], stage_sem.at[c, k, part])

    def own_copy(c, part):
        return pltpu.make_async_copy(share_of(me, c, part), recv.at[c, me, part], own_sem.at[c, part])

    def spectra_copy(c, k):
        return pltpu.make_async_remote_copy(
            src_ref=stage.at[c, k],
            dst_ref=recv.at[c, me],
            send_sem=send_sem.at[c, k],
            recv_sem=recv_sem.at[c, me],
            device_id=(partner(k), g),
            device_id_type=MESH,
        )

    for c in range(chunks):
        for k in turns:
            for part in range(2):
                stage_copy(c, k, part).start()
        for part in range(2):
            own_copy(c, part).start()

    barrier = pltpu.get_barrier_semaphore()
    for t in range(1, n_sta):
        pl.semaphore_signal(
            barrier, inc=1, device_id=(lax.rem(me + t, n_sta), g), device_id_type=MESH
        )
    for t in range(1, n_win):
        pl.semaphore_signal(
            barrier, inc=1, device_id=(me, lax.rem(g + t, n_win)), device_id_type=MESH
        )
    lane = lax.broadcasted_iota(jnp.int32, (1, lab.shape[2]), 1)
    row = jnp.full((1, lab.shape[2]), -2, jnp.int32)
    for r in range(rounds):
        for j in range(stations):
            for i in range(stations):
                row = jnp.where(lane == (r * ROWS + j) * ROWS + i, bins_ref[r, i, j], row)
    lab[pl.ds(me, 1)] = row[None]

    sub = lax.broadcasted_iota(jnp.int32, (n_sta * CAP, LANES), 0)
    slot = jnp.full((n_sta * CAP, LANES), -1, jnp.int32)
    start = jnp.int32(0)
    for o in range(n_sta):
        held = count_ref[o]
        for k in range(CAP):
            chosen = order_ref[jnp.clip(start + k, 0, order_ref.shape[0] - 1)]
            slot = jnp.where(sub == o * CAP + k, jnp.where(k < held, chosen, -1), slot)
        start = start + held
    slots[...] = slot

    wide[...] = jnp.zeros_like(wide)
    pl.semaphore_wait(barrier, n_sta + n_win - 2)

    def label_copy(k):
        return pltpu.make_async_remote_copy(
            src_ref=lab.at[me],
            dst_ref=lab.at[me],
            send_sem=lab_send.at[k],
            recv_sem=lab_recv.at[me],
            device_id=(lax.rem(me + k, n_sta), g),
            device_id_type=MESH,
        )

    for k in range(1, n_sta):
        label_copy(k).start()

    for k in turns:
        for part in range(2):
            stage_copy(0, k, part).wait()
        spectra_copy(0, k).start()

    for c in range(1, chunks):
        for k in turns:
            for part in range(2):
                stage_copy(c, k, part).wait()
            spectra_copy(c - 1, k).wait_send()
            spectra_copy(c, k).start()

    for k in range(1, n_sta):
        src = lax.rem(me - k + n_sta, n_sta)
        pltpu.make_async_remote_copy(
            src_ref=lab.at[src], dst_ref=lab.at[src], send_sem=lab_send.at[k],
            recv_sem=lab_recv.at[src], device_id=(src, g), device_id_type=MESH,
        ).wait_recv()

    def widen(c, p):
        for part in range(2):
            for j in range(stations):
                wide[p, part, pl.ds(j, windows, stride=ROWS), :] = recv[c, p, part, j].astype(jnp.float32)

    def arrive(c, src):
        @pl.when(src != me)
        def _():
            pltpu.make_async_remote_copy(
                src_ref=recv.at[c, src], dst_ref=recv.at[c, src],
                send_sem=send_sem.at[c, 0], recv_sem=recv_sem.at[c, src],
                device_id=(src, g), device_id_type=MESH,
            ).wait_recv()
            widen(c, src)

    def step(p, at_buffer):
        blocks = [lax.rem(p + r, n_sta) for r in range(rounds)]
        re = [[None] * stations for _ in range(rounds)]
        im = [[None] * stations for _ in range(rounds)]
        half = -(-stations // 2)
        for group in (range(half), range(half, stations)):
            for w in range(windows):
                at = pl.ds(w * ROWS, ROWS)
                mine = [(wide[b, 0, at, :], wide[b, 1, at, :]) for b in blocks]
                for j in group:
                    a = wide[p, 0, pl.ds(w * ROWS + j, ROWS, stride=0), :]
                    b = wide[p, 1, pl.ds(w * ROWS + j, ROWS, stride=0), :]
                    for r in range(rounds):
                        x, y = mine[r]
                        if w == 0:
                            re[r][j] = x * a + y * b
                            im[r][j] = y * a - x * b
                        else:
                            re[r][j] = re[r][j] + x * a + y * b
                            im[r][j] = im[r][j] + y * a - x * b
        blank = jnp.zeros((ROWS, LANES), jnp.float32)
        for r in range(rounds):
            at = pl.ds(r * ROWS * ROWS, ROWS * ROWS)
            pad = [blank] * (ROWS - stations)
            crossed[at_buffer, at, 0:LANES] = jnp.concatenate(re[r] + pad, axis=0).astype(jnp.bfloat16)
            crossed[at_buffer, at, LANES:] = jnp.concatenate(im[r] + pad, axis=0).astype(jnp.bfloat16)

    def binned(p, at_buffer):
        blocks = [lax.rem(p + r, n_sta) for r in range(rounds)]
        lanes = lax.broadcasted_iota(jnp.int32, (1, lab.shape[2]), 1)
        names = jnp.full((1, lab.shape[2]), -2, jnp.int32)
        for r in range(rounds):
            names = jnp.where(lanes // (ROWS * ROWS) == r, lab[blocks[r]], names)
        match = jnp.concatenate(
            [slots[...] == names[:, at:at + LANES] for at in range(0, lab.shape[2], LANES)], axis=1
        )
        match = jnp.where(match, 1.0, 0.0).astype(jnp.bfloat16)
        return jnp.dot(match, crossed[at_buffer], preferred_element_type=jnp.float32)

    def box_copies(c, k, part):
        o = partner(k)
        q = part * halves + me // per_out
        t = lax.rem(me, per_out)
        col = pl.multiple_of(t * share + c * LANES, LANES)
        src = outbox.at[c, part, o]
        dst = inbox.at[g, :, pl.ds(col, LANES)]

        def far():
            return pltpu.make_async_remote_copy(
                src_ref=src, dst_ref=dst, send_sem=box_send.at[c, part, k],
                recv_sem=box_recv.at[c, t, g], device_id=(o, q), device_id_type=MESH,
            )

        def near():
            return pltpu.make_async_copy(src, dst, box_recv.at[c, t, g])

        return far, near, q == g

    quarter = n_sta // 4
    place = lax.rem(me, 2 * quarter) // quarter * 2 + lax.rem(me, 2)
    low = me // (n_sta // 2) * (n_sta // 2)
    way = jnp.where(place == 3, -1, 1)
    first = low + jnp.where(place == 3, 1, jnp.where(place == 2, n_sta - 2, 0))

    def block_at(t):
        return lax.rem(first + way * t + 2 * n_sta, n_sta)

    def one_chunk(c, carry):
        for part in range(2):
            own_copy(c, part).wait()
        widen(c, me)
        for r in range(rounds - 1):
            arrive(c, lax.rem(block_at(0) + r + jnp.where(way < 0, 1, 0), n_sta))
        total[...] = jnp.zeros_like(total)
        crossed[...] = jnp.zeros_like(crossed)

        def one_step(t, carry):
            p = block_at(t)

            @pl.when(t <= n_sta - rounds)
            def _():
                arrive(c, lax.rem(p + jnp.where(way < 0, 0, rounds - 1), n_sta))

            now = lax.rem(t, 2)
            total[...] += binned(block_at(t - 1), 1 - now)
            step(p, now)
            return carry

        lax.fori_loop(0, n_sta, one_step, 0)
        total[...] += binned(block_at(n_sta - 1), (n_sta - 1) % 2)
        for part in range(2):
            for o in range(n_sta):
                outbox[c, part, o] = total[o * CAP:(o + 1) * CAP, part * LANES:(part + 1) * LANES]
        for part in range(2):
            for k in range(n_sta):
                far, near, is_me = box_copies(c, k, part)
                if k:
                    far().start()
                else:
                    pl.when(is_me)(lambda near=near: near().start())
                    pl.when(jnp.logical_not(is_me))(lambda far=far: far().start())
        return carry

    lax.fori_loop(0, chunks, one_chunk, 0)

    for c in range(chunks):
        for t in range(per_out):
            for s in range(n_win):
                dst = inbox.at[s, :, pl.ds(t * share + c * LANES, LANES)]
                pltpu.make_async_copy(dst, dst, box_recv.at[c, t, s]).wait()
    out_ref[...] = functools.reduce(jnp.add, [inbox[s] for s in range(n_win)])

    for k in turns:
        spectra_copy(chunks - 1, k).wait_send()
    for c in range(chunks):
        for part in range(2):
            for k in range(n_sta):
                far, near, is_me = box_copies(c, k, part)
                if k:
                    far().wait_send()
                else:
                    pl.when(jnp.logical_not(is_me))(lambda far=far: far().wait_send())
    for k in range(1, n_sta):
        label_copy(k).wait_send()


def by_frequency(spectra, pair_bins, owner_count, bin_order):
    n_sta, n_win = lax.axis_size("sta"), lax.axis_size("win")
    windows, stations, columns = spectra.shape
    rounds = pair_bins.shape[1]
    width = columns // 2
    share = width // n_sta
    chunks = share // LANES
    out_cols = columns // n_win
    per_out = out_cols // share
    depth = -(-rounds * ROWS * ROWS // LANES) * LANES
    sizes = (n_sta, n_win, chunks, windows, stations, rounds, width)
    dma = pltpu.SemaphoreType.DMA
    sums = pl.pallas_call(
        functools.partial(kernel, sizes),
        out_shape=jax.ShapeDtypeStruct((CAP, out_cols), jnp.float32),
        in_specs=[
            pl.BlockSpec(memory_space=pl.ANY),
            pl.BlockSpec(memory_space=pltpu.SMEM),
            pl.BlockSpec(memory_space=pltpu.SMEM),
            pl.BlockSpec(memory_space=pltpu.SMEM),
        ],
        out_specs=pl.BlockSpec(memory_space=pltpu.VMEM),
        scratch_shapes=[
            pltpu.VMEM((chunks, n_sta, 2, stations, windows, LANES), spectra.dtype),
            pltpu.VMEM((chunks, n_sta, 2, stations, windows, LANES), spectra.dtype),
            pltpu.VMEM((n_sta, 2, windows * ROWS, LANES), jnp.float32),
            pltpu.VMEM((n_sta, 1, depth), jnp.int32),
            pltpu.VMEM((n_sta * CAP, LANES), jnp.int32),
            pltpu.VMEM((2, depth, 2 * LANES), jnp.bfloat16),
            pltpu.VMEM((n_sta * CAP, 2 * LANES), jnp.float32),
            pltpu.VMEM((chunks, 2, n_sta, CAP, LANES), jnp.float32),
            pltpu.VMEM((n_win, CAP, out_cols), jnp.float32),
            dma((chunks, n_sta, 2)),
            dma((chunks, n_sta)),
            dma((chunks, n_sta)),
            dma((chunks, 2)),
            dma((n_sta,)),
            dma((n_sta,)),
            dma((chunks, 2, n_sta)),
            dma((chunks, per_out, n_win)),
        ],
        compiler_params=pltpu.CompilerParams(
            collective_id=0, has_side_effects=True, vmem_limit_bytes=56 * 1024 * 1024
        ),
        cost_estimate=pl.CostEstimate(
            flops=8 * width * windows * rounds * stations * stations,
            bytes_accessed=2 * spectra.size, transcendentals=0,
        ),
    )(jnp.transpose(spectra, (1, 0, 2)), jnp.transpose(pair_bins, (1, 0, 2)), owner_count, bin_order)
    return sums * jnp.float32(1.0 / (windows * n_win))


def on_device(spectra, pair_bins, owner_count, bin_order):
    n_sta, n_win = lax.axis_size("sta"), lax.axis_size("win")
    width = spectra.shape[2] // 2
    share, out_cols = width // n_sta, 2 * width // n_win
    fits = (
        width % (n_sta * LANES) == 0 and out_cols % share == 0 and width % out_cols == 0
        and spectra.shape[1] <= ROWS and pair_bins.shape[1] <= n_sta - 1
    )
    plan = by_frequency if fits else by_blocks
    return plan(spectra, pair_bins, owner_count, bin_order)


def solution(mesh):
    return jax.shard_map(
        on_device,
        mesh=mesh,
        in_specs=(P("win", "sta", None), P("sta", None, None), P(), P()),
        out_specs=P("sta", "win"),
        check_vma=False,
    )
```

```python
import functools
import jax
import jax.numpy as jnp
from jax import lax
from jax.experimental import pallas as pl
from jax.experimental.pallas import tpu as pltpu
from jax.sharding import PartitionSpec as P

CAP = 4
LANES = 128
ROWS = 8
MESH = pl.DeviceIdType.MESH


def passed_along(value, axis, steps):
    count = lax.axis_size(axis)
    pairs = [(source, (source + steps) % count) for source in range(count)]
    return lax.ppermute(value, axis, pairs)


def cross_pairs(own, other):
    width = own.shape[-1] // 2
    own_re, own_im = (own[..., :width], own[..., width:])
    other_re, other_im = (other[..., :width], other[..., width:])
    form = "wsf,wtf->stf"
    real = jnp.einsum(form, own_re, other_re, preferred_element_type=jnp.float32) + jnp.einsum(
        form, own_im, other_im, preferred_element_type=jnp.float32
    )
    imag = jnp.einsum(form, own_im, other_re, preferred_element_type=jnp.float32) - jnp.einsum(
        form, own_re, other_im, preferred_element_type=jnp.float32
    )
    joined = jnp.concatenate([real, imag], axis=-1).astype(jnp.bfloat16)
    return joined.reshape(-1, joined.shape[-1])


def by_blocks(spectra, pair_bins, owner_count, bin_order):
    rounds = pair_bins.shape[1]
    blocks = [spectra]
    for offset in range(1, rounds):
        blocks.append(passed_along(spectra, "sta", offset))
    crossed = jnp.concatenate([cross_pairs(spectra, other) for other in blocks], axis=0)
    labels = jnp.transpose(pair_bins, (1, 0, 2)).reshape(-1)
    bin_total = bin_order.shape[0]
    starts = jnp.cumsum(owner_count) - owner_count
    ranks = jnp.arange(CAP, dtype=jnp.int32)
    positions = jnp.clip(starts[:, None] + ranks[None, :], 0, bin_total - 1)
    valid = ranks[None, :] < owner_count[:, None]
    chosen = jnp.take(bin_order, positions)
    slot_bin = jnp.where(valid, chosen, -1).reshape(-1)
    window_total = spectra.shape[0] * lax.axis_size("win")
    matches = (slot_bin[:, None] == labels[None, :]).astype(jnp.bfloat16)
    partial_sums = jnp.dot(matches, crossed, preferred_element_type=jnp.float32)
    spread = lax.psum_scatter(partial_sums, "win", scatter_dimension=1, tiled=True)
    stacks = lax.psum_scatter(spread, "sta", scatter_dimension=0, tiled=True)
    return stacks * jnp.float32(1.0 / window_total)


def kernel(
    sizes, spec_ref, bins_ref, count_ref, order_ref, out_ref,
    stage, recv, wide, lab, slots, crossed, total, outbox, inbox,
    stage_sem, send_sem, recv_sem, own_sem, lab_send, lab_recv, box_send, box_recv,
):
    n_sta, n_win, chunks, windows, stations, rounds, width = sizes
    share = width // n_sta
    out_cols = out_ref.shape[1]
    per_out = out_cols // share
    halves = width // out_cols
    me = lax.axis_index("sta")
    g = lax.axis_index("win")

    def partner(k):
        if n_sta & (n_sta - 1):
            return lax.rem(me + k, n_sta)
        digits, bit = me, 1
        while bit < n_sta:
            if k & bit:
                digits = digits + bit - 2 * bit * lax.rem(digits // bit, 2)
            bit *= 2
        return digits

    far_half = list(range(n_sta // 2, n_sta))
    near_half = list(range(1, n_sta // 2)) + [None]
    turns = [k for pair in zip(far_half, near_half) for k in pair if k is not None]

    def share_of(dest, c, part):
        col = pl.multiple_of(part * width + dest * share + c * LANES, LANES)
        return spec_ref.at[:, :, pl.ds(col, LANES)]

    def stage_copy(c, k, part):
        return pltpu.make_async_copy(share_of(partner(k), c, part), stage.at[c, k, part], stage_sem.at[c, k, part])

    def own_copy(c, part):
        return pltpu.make_async_copy(share_of(me, c, part), recv.at[c, me, part], own_sem.at[c, part])

    def spectra_copy(c, k):
        return pltpu.make_async_remote_copy(
            src_ref=stage.at[c, k],
            dst_ref=recv.at[c, me],
            send_sem=send_sem.at[c, k],
            recv_sem=recv_sem.at[c, me],
            device_id=(partner(k), g),
            device_id_type=MESH,
        )

    for c in range(chunks):
        for k in turns:
            for part in range(2):
                stage_copy(c, k, part).start()
        for part in range(2):
            own_copy(c, part).start()

    barrier = pltpu.get_barrier_semaphore()
    for t in range(1, n_sta):
        pl.semaphore_signal(
            barrier, inc=1, device_id=(lax.rem(me + t, n_sta), g), device_id_type=MESH
        )
    for t in range(1, n_win):
        pl.semaphore_signal(
            barrier, inc=1, device_id=(me, lax.rem(g + t, n_win)), device_id_type=MESH
        )
    lane = lax.broadcasted_iota(jnp.int32, (1, lab.shape[2]), 1)
    row = jnp.full((1, lab.shape[2]), -2, jnp.int32)
    for r in range(rounds):
        for j in range(stations):
            for i in range(stations):
                row = jnp.where(lane == (r * ROWS + j) * ROWS + i, bins_ref[r, i, j], row)
    lab[pl.ds(me, 1)] = row[None]

    sub = lax.broadcasted_iota(jnp.int32, (n_sta * CAP, LANES), 0)
    slot = jnp.full((n_sta * CAP, LANES), -1, jnp.int32)
    start = jnp.int32(0)
    for o in range(n_sta):
        held = count_ref[o]
        for k in range(CAP):
            chosen = order_ref[jnp.clip(start + k, 0, order_ref.shape[0] - 1)]
            slot = jnp.where(sub == o * CAP + k, jnp.where(k < held, chosen, -1), slot)
        start = start + held
    slots[...] = slot

    wide[...] = jnp.zeros_like(wide)
    pl.semaphore_wait(barrier, n_sta + n_win - 2)

    def label_copy(k):
        return pltpu.make_async_remote_copy(
            src_ref=lab.at[me],
            dst_ref=lab.at[me],
            send_sem=lab_send.at[k],
            recv_sem=lab_recv.at[me],
            device_id=(lax.rem(me + k, n_sta), g),
            device_id_type=MESH,
        )

    for k in range(1, n_sta):
        label_copy(k).start()

    for k in turns:
        for part in range(2):
            stage_copy(0, k, part).wait()
        spectra_copy(0, k).start()

    for c in range(1, chunks):
        for k in turns:
            for part in range(2):
                stage_copy(c, k, part).wait()
            spectra_copy(c, k).start()

    for k in range(1, n_sta):
        src = lax.rem(me - k + n_sta, n_sta)
        pltpu.make_async_remote_copy(
            src_ref=lab.at[src], dst_ref=lab.at[src], send_sem=lab_send.at[k],
            recv_sem=lab_recv.at[src], device_id=(src, g), device_id_type=MESH,
        ).wait_recv()

    def widen(c, p):
        for part in range(2):
            for j in range(stations):
                wide[p, part, pl.ds(j, windows, stride=ROWS), :] = recv[c, p, part, j].astype(jnp.float32)

    def arrive(c, src):
        @pl.when(src != me)
        def _():
            pltpu.make_async_remote_copy(
                src_ref=recv.at[c, src], dst_ref=recv.at[c, src],
                send_sem=send_sem.at[c, 0], recv_sem=recv_sem.at[c, src],
                device_id=(src, g), device_id_type=MESH,
            ).wait_recv()
            widen(c, src)

    def step(p, at_buffer):
        blocks = [lax.rem(p + r, n_sta) for r in range(rounds)]
        re = [[None] * stations for _ in range(rounds)]
        im = [[None] * stations for _ in range(rounds)]
        half = -(-stations // 2)
        for group in (range(half), range(half, stations)):
            for w in range(windows):
                at = pl.ds(w * ROWS, ROWS)
                mine = [(wide[b, 0, at, :], wide[b, 1, at, :]) for b in blocks]
                for j in group:
                    a = wide[p, 0, pl.ds(w * ROWS + j, ROWS, stride=0), :]
                    b = wide[p, 1, pl.ds(w * ROWS + j, ROWS, stride=0), :]
                    for r in range(rounds):
                        x, y = mine[r]
                        if w == 0:
                            re[r][j] = x * a + y * b
                            im[r][j] = y * a - x * b
                        else:
                            re[r][j] = re[r][j] + x * a + y * b
                            im[r][j] = im[r][j] + y * a - x * b
        blank = jnp.zeros((ROWS, LANES), jnp.float32)
        for r in range(rounds):
            at = pl.ds(r * ROWS * ROWS, ROWS * ROWS)
            pad = [blank] * (ROWS - stations)
            crossed[at_buffer, at, 0:LANES] = jnp.concatenate(re[r] + pad, axis=0).astype(jnp.bfloat16)
            crossed[at_buffer, at, LANES:] = jnp.concatenate(im[r] + pad, axis=0).astype(jnp.bfloat16)

    def binned(p, at_buffer):
        blocks = [lax.rem(p + r, n_sta) for r in range(rounds)]
        lanes = lax.broadcasted_iota(jnp.int32, (1, lab.shape[2]), 1)
        names = jnp.full((1, lab.shape[2]), -2, jnp.int32)
        for r in range(rounds):
            names = jnp.where(lanes // (ROWS * ROWS) == r, lab[blocks[r]], names)
        match = jnp.concatenate(
            [slots[...] == names[:, at:at + LANES] for at in range(0, lab.shape[2], LANES)], axis=1
        )
        match = jnp.where(match, 1.0, 0.0).astype(jnp.bfloat16)
        return jnp.dot(match, crossed[at_buffer], preferred_element_type=jnp.float32)

    def box_copies(c, k, part):
        o = partner(k)
        q = part * halves + me // per_out
        t = lax.rem(me, per_out)
        col = pl.multiple_of(t * share + c * LANES, LANES)
        src = outbox.at[c, part, o]
        dst = inbox.at[g, :, pl.ds(col, LANES)]

        def far():
            return pltpu.make_async_remote_copy(
                src_ref=src, dst_ref=dst, send_sem=box_send.at[c, part, k],
                recv_sem=box_recv.at[c, t, g], device_id=(o, q), device_id_type=MESH,
            )

        def near():
            return pltpu.make_async_copy(src, dst, box_recv.at[c, t, g])

        return far, near, q == g

    quarter = n_sta // 4
    place = lax.rem(me, 2 * quarter) // quarter * 2 + lax.rem(me, 2)
    low = me // (n_sta // 2) * (n_sta // 2)
    way = jnp.where(place == 3, -1, 1)
    first = low + jnp.where(place == 3, 1, jnp.where(place == 2, n_sta - 2, 0))

    def block_at(t):
        return lax.rem(first + way * t + 2 * n_sta, n_sta)

    def one_chunk(c, carry):
        for part in range(2):
            own_copy(c, part).wait()
        widen(c, me)
        for r in range(rounds - 1):
            arrive(c, lax.rem(block_at(0) + r + jnp.where(way < 0, 1, 0), n_sta))
        total[...] = jnp.zeros_like(total)
        crossed[...] = jnp.zeros_like(crossed)

        def one_step(t, carry):
            p = block_at(t)

            @pl.when(t <= n_sta - rounds)
            def _():
                arrive(c, lax.rem(p + jnp.where(way < 0, 0, rounds - 1), n_sta))

            now = lax.rem(t, 2)
            total[...] += binned(block_at(t - 1), 1 - now)
            step(p, now)
            return carry

        lax.fori_loop(0, n_sta, one_step, 0)
        total[...] += binned(block_at(n_sta - 1), (n_sta - 1) % 2)
        for part in range(2):
            for o in range(n_sta):
                outbox[c, part, o] = total[o * CAP:(o + 1) * CAP, part * LANES:(part + 1) * LANES]
        for part in range(2):
            for k in range(n_sta):
                far, near, is_me = box_copies(c, k, part)
                if k:
                    far().start()
                else:
                    pl.when(is_me)(lambda near=near: near().start())
                    pl.when(jnp.logical_not(is_me))(lambda far=far: far().start())
        return carry

    lax.fori_loop(0, chunks, one_chunk, 0)

    for c in range(chunks):
        for t in range(per_out):
            for s in range(n_win):
                dst = inbox.at[s, :, pl.ds(t * share + c * LANES, LANES)]
                pltpu.make_async_copy(dst, dst, box_recv.at[c, t, s]).wait()
    out_ref[...] = functools.reduce(jnp.add, [inbox[s] for s in range(n_win)])

    for c in range(chunks):
        for k in turns:
            spectra_copy(c, k).wait_send()
    for c in range(chunks):
        for part in range(2):
            for k in range(n_sta):
                far, near, is_me = box_copies(c, k, part)
                if k:
                    far().wait_send()
                else:
                    pl.when(jnp.logical_not(is_me))(lambda far=far: far().wait_send())
    for k in range(1, n_sta):
        label_copy(k).wait_send()


def by_frequency(spectra, pair_bins, owner_count, bin_order):
    n_sta, n_win = lax.axis_size("sta"), lax.axis_size("win")
    windows, stations, columns = spectra.shape
    rounds = pair_bins.shape[1]
    width = columns // 2
    share = width // n_sta
    chunks = share // LANES
    out_cols = columns // n_win
    per_out = out_cols // share
    depth = -(-rounds * ROWS * ROWS // LANES) * LANES
    sizes = (n_sta, n_win, chunks, windows, stations, rounds, width)
    dma = pltpu.SemaphoreType.DMA
    sums = pl.pallas_call(
        functools.partial(kernel, sizes),
        out_shape=jax.ShapeDtypeStruct((CAP, out_cols), jnp.float32),
        in_specs=[
            pl.BlockSpec(memory_space=pl.ANY),
            pl.BlockSpec(memory_space=pltpu.SMEM),
            pl.BlockSpec(memory_space=pltpu.SMEM),
            pl.BlockSpec(memory_space=pltpu.SMEM),
        ],
        out_specs=pl.BlockSpec(memory_space=pltpu.VMEM),
        scratch_shapes=[
            pltpu.VMEM((chunks, n_sta, 2, stations, windows, LANES), spectra.dtype),
            pltpu.VMEM((chunks, n_sta, 2, stations, windows, LANES), spectra.dtype),
            pltpu.VMEM((n_sta, 2, windows * ROWS, LANES), jnp.float32),
            pltpu.VMEM((n_sta, 1, depth), jnp.int32),
            pltpu.VMEM((n_sta * CAP, LANES), jnp.int32),
            pltpu.VMEM((2, depth, 2 * LANES), jnp.bfloat16),
            pltpu.VMEM((n_sta * CAP, 2 * LANES), jnp.float32),
            pltpu.VMEM((chunks, 2, n_sta, CAP, LANES), jnp.float32),
            pltpu.VMEM((n_win, CAP, out_cols), jnp.float32),
            dma((chunks, n_sta, 2)),
            dma((chunks, n_sta)),
            dma((chunks, n_sta)),
            dma((chunks, 2)),
            dma((n_sta,)),
            dma((n_sta,)),
            dma((chunks, 2, n_sta)),
            dma((chunks, per_out, n_win)),
        ],
        compiler_params=pltpu.CompilerParams(
            collective_id=0, has_side_effects=True, vmem_limit_bytes=56 * 1024 * 1024
        ),
        cost_estimate=pl.CostEstimate(
            flops=8 * width * windows * rounds * stations * stations,
            bytes_accessed=2 * spectra.size, transcendentals=0,
        ),
    )(jnp.transpose(spectra, (1, 0, 2)), jnp.transpose(pair_bins, (1, 0, 2)), owner_count, bin_order)
    return sums * jnp.float32(1.0 / (windows * n_win))


def on_device(spectra, pair_bins, owner_count, bin_order):
    n_sta, n_win = lax.axis_size("sta"), lax.axis_size("win")
    width = spectra.shape[2] // 2
    share, out_cols = width // n_sta, 2 * width // n_win
    fits = (
        width % (n_sta * LANES) == 0 and out_cols % share == 0 and width % out_cols == 0
        and spectra.shape[1] <= ROWS and pair_bins.shape[1] <= n_sta - 1
    )
    plan = by_frequency if fits else by_blocks
    return plan(spectra, pair_bins, owner_count, bin_order)


def solution(mesh):
    return jax.shard_map(
        on_device,
        mesh=mesh,
        in_specs=(P("win", "sta", None), P("sta", None, None), P(), P()),
        out_specs=P("sta", "win"),
        check_vma=False,
    )
```

```python
import functools
import jax
import jax.numpy as jnp
from jax import lax
from jax.experimental import pallas as pl
from jax.experimental.pallas import tpu as pltpu
from jax.sharding import PartitionSpec as P

CAP = 4
LANES = 128
ROWS = 8
MESH = pl.DeviceIdType.MESH


def passed_along(value, axis, steps):
    count = lax.axis_size(axis)
    pairs = [(source, (source + steps) % count) for source in range(count)]
    return lax.ppermute(value, axis, pairs)


def cross_pairs(own, other):
    width = own.shape[-1] // 2
    own_re, own_im = (own[..., :width], own[..., width:])
    other_re, other_im = (other[..., :width], other[..., width:])
    form = "wsf,wtf->stf"
    real = jnp.einsum(form, own_re, other_re, preferred_element_type=jnp.float32) + jnp.einsum(
        form, own_im, other_im, preferred_element_type=jnp.float32
    )
    imag = jnp.einsum(form, own_im, other_re, preferred_element_type=jnp.float32) - jnp.einsum(
        form, own_re, other_im, preferred_element_type=jnp.float32
    )
    joined = jnp.concatenate([real, imag], axis=-1).astype(jnp.bfloat16)
    return joined.reshape(-1, joined.shape[-1])


def by_blocks(spectra, pair_bins, owner_count, bin_order):
    rounds = pair_bins.shape[1]
    blocks = [spectra]
    for offset in range(1, rounds):
        blocks.append(passed_along(spectra, "sta", offset))
    crossed = jnp.concatenate([cross_pairs(spectra, other) for other in blocks], axis=0)
    labels = jnp.transpose(pair_bins, (1, 0, 2)).reshape(-1)
    bin_total = bin_order.shape[0]
    starts = jnp.cumsum(owner_count) - owner_count
    ranks = jnp.arange(CAP, dtype=jnp.int32)
    positions = jnp.clip(starts[:, None] + ranks[None, :], 0, bin_total - 1)
    valid = ranks[None, :] < owner_count[:, None]
    chosen = jnp.take(bin_order, positions)
    slot_bin = jnp.where(valid, chosen, -1).reshape(-1)
    window_total = spectra.shape[0] * lax.axis_size("win")
    matches = (slot_bin[:, None] == labels[None, :]).astype(jnp.bfloat16)
    partial_sums = jnp.dot(matches, crossed, preferred_element_type=jnp.float32)
    spread = lax.psum_scatter(partial_sums, "win", scatter_dimension=1, tiled=True)
    stacks = lax.psum_scatter(spread, "sta", scatter_dimension=0, tiled=True)
    return stacks * jnp.float32(1.0 / window_total)


def kernel(
    sizes, spec_ref, bins_ref, count_ref, order_ref, out_ref,
    stage, recv, wide, lab, slots, crossed, total, outbox, inbox,
    stage_sem, send_sem, recv_sem, own_sem, lab_send, lab_recv, box_send, box_recv,
):
    n_sta, n_win, chunks, windows, stations, rounds, width = sizes
    share = width // n_sta
    out_cols = out_ref.shape[1]
    per_out = out_cols // share
    halves = width // out_cols
    me = lax.axis_index("sta")
    g = lax.axis_index("win")

    def partner(k):
        if n_sta & (n_sta - 1):
            return lax.rem(me + k, n_sta)
        digits, bit = me, 1
        while bit < n_sta:
            if k & bit:
                digits = digits + bit - 2 * bit * lax.rem(digits // bit, 2)
            bit *= 2
        return digits

    far_half = list(range(n_sta // 2, n_sta))
    near_half = list(range(1, n_sta // 2)) + [None]
    turns = [k for pair in zip(far_half, near_half) for k in pair if k is not None]

    def share_of(dest, c, part):
        col = pl.multiple_of(part * width + dest * share + c * LANES, LANES)
        return spec_ref.at[:, :, pl.ds(col, LANES)]

    def stage_copy(c, k, part):
        return pltpu.make_async_copy(share_of(partner(k), c, part), stage.at[c, k, part], stage_sem.at[c, k, part])

    def own_copy(c, part):
        return pltpu.make_async_copy(share_of(me, c, part), recv.at[c, me, part], own_sem.at[c, part])

    def spectra_copy(c, k):
        return pltpu.make_async_remote_copy(
            src_ref=stage.at[c, k],
            dst_ref=recv.at[c, me],
            send_sem=send_sem.at[c, k],
            recv_sem=recv_sem.at[c, me],
            device_id=(partner(k), g),
            device_id_type=MESH,
        )

    for c in range(chunks):
        for k in turns:
            for part in range(2):
                stage_copy(c, k, part).start()
        for part in range(2):
            own_copy(c, part).start()

    barrier = pltpu.get_barrier_semaphore()
    for t in range(1, n_sta):
        pl.semaphore_signal(
            barrier, inc=1, device_id=(lax.rem(me + t, n_sta), g), device_id_type=MESH
        )
    for t in range(1, n_win):
        pl.semaphore_signal(
            barrier, inc=1, device_id=(me, lax.rem(g + t, n_win)), device_id_type=MESH
        )
    lane = lax.broadcasted_iota(jnp.int32, (1, lab.shape[2]), 1)
    row = jnp.full((1, lab.shape[2]), -2, jnp.int32)
    for r in range(rounds):
        for j in range(stations):
            for i in range(stations):
                row = jnp.where(lane == (r * ROWS + j) * ROWS + i, bins_ref[r, i, j], row)
    lab[pl.ds(me, 1)] = row[None]

    sub = lax.broadcasted_iota(jnp.int32, (n_sta * CAP, LANES), 0)
    slot = jnp.full((n_sta * CAP, LANES), -1, jnp.int32)
    start = jnp.int32(0)
    for o in range(n_sta):
        held = count_ref[o]
        for k in range(CAP):
            chosen = order_ref[jnp.clip(start + k, 0, order_ref.shape[0] - 1)]
            slot = jnp.where(sub == o * CAP + k, jnp.where(k < held, chosen, -1), slot)
        start = start + held
    slots[...] = slot

    wide[...] = jnp.zeros_like(wide)
    pl.semaphore_wait(barrier, n_sta + n_win - 2)

    def label_copy(k):
        return pltpu.make_async_remote_copy(
            src_ref=lab.at[me],
            dst_ref=lab.at[me],
            send_sem=lab_send.at[k],
            recv_sem=lab_recv.at[me],
            device_id=(lax.rem(me + k, n_sta), g),
            device_id_type=MESH,
        )

    for k in range(1, n_sta):
        label_copy(k).start()

    for k in turns:
        for part in range(2):
            stage_copy(0, k, part).wait()
        spectra_copy(0, k).start()

    for c in range(1, chunks):
        for k in turns:
            for part in range(2):
                stage_copy(c, k, part).wait()
            spectra_copy(c, k).start()

    for k in range(1, n_sta):
        src = lax.rem(me - k + n_sta, n_sta)
        pltpu.make_async_remote_copy(
            src_ref=lab.at[src], dst_ref=lab.at[src], send_sem=lab_send.at[k],
            recv_sem=lab_recv.at[src], device_id=(src, g), device_id_type=MESH,
        ).wait_recv()

    def widen(c, p):
        for j in range(stations):
            x = recv[c, p, 0, j].astype(jnp.float32)
            y = recv[c, p, 1, j].astype(jnp.float32)
            for part, value in enumerate((x, y, x + y, x - y)):
                wide[p, part, pl.ds(j, windows, stride=ROWS), :] = value

    def arrive(c, src):
        @pl.when(src != me)
        def _():
            pltpu.make_async_remote_copy(
                src_ref=recv.at[c, src], dst_ref=recv.at[c, src],
                send_sem=send_sem.at[c, 0], recv_sem=recv_sem.at[c, src],
                device_id=(src, g), device_id_type=MESH,
            ).wait_recv()
            widen(c, src)

    def step(p, at_buffer):
        blocks = [lax.rem(p + r, n_sta) for r in range(rounds)]
        both = [[None] * stations for _ in range(rounds)]
        minus_re = [[None] * stations for _ in range(rounds)]
        minus_im = [[None] * stations for _ in range(rounds)]
        half = -(-stations // 2)
        for group in (range(half), range(half, stations)):
            for w in range(windows):
                at = pl.ds(w * ROWS, ROWS)
                mine = [[wide[b, part, at, :] for part in range(3)] for b in blocks]
                for j in group:
                    a, a_plus_b, a_minus_b = [
                        wide[p, part, pl.ds(w * ROWS + j, ROWS, stride=0), :] for part in (0, 2, 3)
                    ]
                    for r in range(rounds):
                        x, y, x_plus_y = mine[r]
                        terms = (a * x_plus_y, y * a_minus_b, x * a_plus_b)
                        for sums, term in zip((both, minus_re, minus_im), terms):
                            sums[r][j] = term if w == 0 else sums[r][j] + term
        re = [[u - v for u, v in zip(both[r], minus_re[r])] for r in range(rounds)]
        im = [[u - v for u, v in zip(both[r], minus_im[r])] for r in range(rounds)]
        blank = jnp.zeros((ROWS, LANES), jnp.float32)
        for r in range(rounds):
            at = pl.ds(r * ROWS * ROWS, ROWS * ROWS)
            pad = [blank] * (ROWS - stations)
            crossed[at_buffer, at, 0:LANES] = jnp.concatenate(re[r] + pad, axis=0).astype(jnp.bfloat16)
            crossed[at_buffer, at, LANES:] = jnp.concatenate(im[r] + pad, axis=0).astype(jnp.bfloat16)

    def binned(p, at_buffer):
        blocks = [lax.rem(p + r, n_sta) for r in range(rounds)]
        lanes = lax.broadcasted_iota(jnp.int32, (1, lab.shape[2]), 1)
        names = jnp.full((1, lab.shape[2]), -2, jnp.int32)
        for r in range(rounds):
            names = jnp.where(lanes // (ROWS * ROWS) == r, lab[blocks[r]], names)
        match = jnp.concatenate(
            [slots[...] == names[:, at:at + LANES] for at in range(0, lab.shape[2], LANES)], axis=1
        )
        match = jnp.where(match, 1.0, 0.0).astype(jnp.bfloat16)
        return jnp.dot(match, crossed[at_buffer], preferred_element_type=jnp.float32)

    def box_copies(c, k, part):
        o = partner(k)
        q = part * halves + me // per_out
        t = lax.rem(me, per_out)
        col = pl.multiple_of(t * share + c * LANES, LANES)
        src = outbox.at[c, part, o]
        dst = inbox.at[g, :, pl.ds(col, LANES)]

        def far():
            return pltpu.make_async_remote_copy(
                src_ref=src, dst_ref=dst, send_sem=box_send.at[c, part, k],
                recv_sem=box_recv.at[c, t, g], device_id=(o, q), device_id_type=MESH,
            )

        def near():
            return pltpu.make_async_copy(src, dst, box_recv.at[c, t, g])

        return far, near, q == g

    quarter = n_sta // 4
    place = lax.rem(me, 2 * quarter) // quarter * 2 + lax.rem(me, 2)
    low = me // (n_sta // 2) * (n_sta // 2)
    way = jnp.where(place == 3, -1, 1)
    first = low + jnp.where(place == 3, 1, jnp.where(place == 2, n_sta - 2, 0))

    def block_at(t):
        return lax.rem(first + way * t + 2 * n_sta, n_sta)

    def one_chunk(c, carry):
        for part in range(2):
            own_copy(c, part).wait()
        widen(c, me)
        for r in range(rounds - 1):
            arrive(c, lax.rem(block_at(0) + r + jnp.where(way < 0, 1, 0), n_sta))
        total[...] = jnp.zeros_like(total)
        crossed[...] = jnp.zeros_like(crossed)

        def one_step(t, carry):
            p = block_at(t)

            @pl.when(t <= n_sta - rounds)
            def _():
                arrive(c, lax.rem(p + jnp.where(way < 0, 0, rounds - 1), n_sta))

            now = lax.rem(t, 2)
            total[...] += binned(block_at(t - 1), 1 - now)
            step(p, now)
            return carry

        lax.fori_loop(0, n_sta, one_step, 0)
        total[...] += binned(block_at(n_sta - 1), (n_sta - 1) % 2)
        for part in range(2):
            for o in range(n_sta):
                outbox[c, part, o] = total[o * CAP:(o + 1) * CAP, part * LANES:(part + 1) * LANES]
        for part in range(2):
            for k in range(n_sta):
                far, near, is_me = box_copies(c, k, part)
                if k:
                    far().start()
                else:
                    pl.when(is_me)(lambda near=near: near().start())
                    pl.when(jnp.logical_not(is_me))(lambda far=far: far().start())
        return carry

    lax.fori_loop(0, chunks, one_chunk, 0)

    for c in range(chunks):
        for t in range(per_out):
            for s in range(n_win):
                dst = inbox.at[s, :, pl.ds(t * share + c * LANES, LANES)]
                pltpu.make_async_copy(dst, dst, box_recv.at[c, t, s]).wait()
    out_ref[...] = functools.reduce(jnp.add, [inbox[s] for s in range(n_win)])

    for c in range(chunks):
        for k in turns:
            spectra_copy(c, k).wait_send()
    for c in range(chunks):
        for part in range(2):
            for k in range(n_sta):
                far, near, is_me = box_copies(c, k, part)
                if k:
                    far().wait_send()
                else:
                    pl.when(jnp.logical_not(is_me))(lambda far=far: far().wait_send())
    for k in range(1, n_sta):
        label_copy(k).wait_send()


def by_frequency(spectra, pair_bins, owner_count, bin_order):
    n_sta, n_win = lax.axis_size("sta"), lax.axis_size("win")
    windows, stations, columns = spectra.shape
    rounds = pair_bins.shape[1]
    width = columns // 2
    share = width // n_sta
    chunks = share // LANES
    out_cols = columns // n_win
    per_out = out_cols // share
    depth = -(-rounds * ROWS * ROWS // LANES) * LANES
    sizes = (n_sta, n_win, chunks, windows, stations, rounds, width)
    dma = pltpu.SemaphoreType.DMA
    sums = pl.pallas_call(
        functools.partial(kernel, sizes),
        out_shape=jax.ShapeDtypeStruct((CAP, out_cols), jnp.float32),
        in_specs=[
            pl.BlockSpec(memory_space=pl.ANY),
            pl.BlockSpec(memory_space=pltpu.SMEM),
            pl.BlockSpec(memory_space=pltpu.SMEM),
            pl.BlockSpec(memory_space=pltpu.SMEM),
        ],
        out_specs=pl.BlockSpec(memory_space=pltpu.VMEM),
        scratch_shapes=[
            pltpu.VMEM((chunks, n_sta, 2, stations, windows, LANES), spectra.dtype),
            pltpu.VMEM((chunks, n_sta, 2, stations, windows, LANES), spectra.dtype),
            pltpu.VMEM((n_sta, 4, windows * ROWS, LANES), jnp.float32),
            pltpu.VMEM((n_sta, 1, depth), jnp.int32),
            pltpu.VMEM((n_sta * CAP, LANES), jnp.int32),
            pltpu.VMEM((2, depth, 2 * LANES), jnp.bfloat16),
            pltpu.VMEM((n_sta * CAP, 2 * LANES), jnp.float32),
            pltpu.VMEM((chunks, 2, n_sta, CAP, LANES), jnp.float32),
            pltpu.VMEM((n_win, CAP, out_cols), jnp.float32),
            dma((chunks, n_sta, 2)),
            dma((chunks, n_sta)),
            dma((chunks, n_sta)),
            dma((chunks, 2)),
            dma((n_sta,)),
            dma((n_sta,)),
            dma((chunks, 2, n_sta)),
            dma((chunks, per_out, n_win)),
        ],
        compiler_params=pltpu.CompilerParams(
            collective_id=0, has_side_effects=True, vmem_limit_bytes=56 * 1024 * 1024
        ),
        cost_estimate=pl.CostEstimate(
            flops=8 * width * windows * rounds * stations * stations,
            bytes_accessed=2 * spectra.size, transcendentals=0,
        ),
    )(jnp.transpose(spectra, (1, 0, 2)), jnp.transpose(pair_bins, (1, 0, 2)), owner_count, bin_order)
    return sums * jnp.float32(1.0 / (windows * n_win))


def on_device(spectra, pair_bins, owner_count, bin_order):
    n_sta, n_win = lax.axis_size("sta"), lax.axis_size("win")
    width = spectra.shape[2] // 2
    share, out_cols = width // n_sta, 2 * width // n_win
    fits = (
        width % (n_sta * LANES) == 0 and out_cols % share == 0 and width % out_cols == 0
        and spectra.shape[1] <= ROWS and pair_bins.shape[1] <= n_sta - 1
    )
    plan = by_frequency if fits else by_blocks
    return plan(spectra, pair_bins, owner_count, bin_order)


def solution(mesh):
    return jax.shard_map(
        on_device,
        mesh=mesh,
        in_specs=(P("win", "sta", None), P("sta", None, None), P(), P()),
        out_specs=P("sta", "win"),
        check_vma=False,
    )
```

```python
import functools
import jax
import jax.numpy as jnp
from jax import lax
from jax.experimental import pallas as pl
from jax.experimental.pallas import tpu as pltpu
from jax.sharding import PartitionSpec as P

CAP = 4
LANES = 128
ROWS = 8
MESH = pl.DeviceIdType.MESH


def passed_along(value, axis, steps):
    count = lax.axis_size(axis)
    pairs = [(source, (source + steps) % count) for source in range(count)]
    return lax.ppermute(value, axis, pairs)


def cross_pairs(own, other):
    width = own.shape[-1] // 2
    own_re, own_im = (own[..., :width], own[..., width:])
    other_re, other_im = (other[..., :width], other[..., width:])
    form = "wsf,wtf->stf"
    real = jnp.einsum(form, own_re, other_re, preferred_element_type=jnp.float32) + jnp.einsum(
        form, own_im, other_im, preferred_element_type=jnp.float32
    )
    imag = jnp.einsum(form, own_im, other_re, preferred_element_type=jnp.float32) - jnp.einsum(
        form, own_re, other_im, preferred_element_type=jnp.float32
    )
    joined = jnp.concatenate([real, imag], axis=-1).astype(jnp.bfloat16)
    return joined.reshape(-1, joined.shape[-1])


def by_blocks(spectra, pair_bins, owner_count, bin_order):
    rounds = pair_bins.shape[1]
    blocks = [spectra]
    for offset in range(1, rounds):
        blocks.append(passed_along(spectra, "sta", offset))
    crossed = jnp.concatenate([cross_pairs(spectra, other) for other in blocks], axis=0)
    labels = jnp.transpose(pair_bins, (1, 0, 2)).reshape(-1)
    bin_total = bin_order.shape[0]
    starts = jnp.cumsum(owner_count) - owner_count
    ranks = jnp.arange(CAP, dtype=jnp.int32)
    positions = jnp.clip(starts[:, None] + ranks[None, :], 0, bin_total - 1)
    valid = ranks[None, :] < owner_count[:, None]
    chosen = jnp.take(bin_order, positions)
    slot_bin = jnp.where(valid, chosen, -1).reshape(-1)
    window_total = spectra.shape[0] * lax.axis_size("win")
    matches = (slot_bin[:, None] == labels[None, :]).astype(jnp.bfloat16)
    partial_sums = jnp.dot(matches, crossed, preferred_element_type=jnp.float32)
    spread = lax.psum_scatter(partial_sums, "win", scatter_dimension=1, tiled=True)
    stacks = lax.psum_scatter(spread, "sta", scatter_dimension=0, tiled=True)
    return stacks * jnp.float32(1.0 / window_total)


def kernel(
    sizes, spec_ref, bins_ref, count_ref, order_ref, out_ref,
    stage, recv, wide, lab, slots, crossed, total, outbox, inbox,
    stage_sem, send_sem, recv_sem, own_sem, lab_send, lab_recv, box_send, box_recv,
):
    n_sta, n_win, chunks, windows, stations, rounds, width = sizes
    share = width // n_sta
    out_cols = out_ref.shape[1]
    per_out = out_cols // share
    halves = width // out_cols
    me = lax.axis_index("sta")
    g = lax.axis_index("win")

    def partner(k):
        if n_sta & (n_sta - 1):
            return lax.rem(me + k, n_sta)
        digits, bit = me, 1
        while bit < n_sta:
            of_me, of_k = lax.rem(me // bit, 2), lax.rem(k // bit, 2)
            digits = digits + bit * of_k * (1 - 2 * of_me)
            bit *= 2
        return digits

    far_half = list(range(n_sta // 2, n_sta))
    near_half = list(range(1, n_sta // 2))
    even = [k for pair in zip(far_half, near_half) for k in pair] + far_half[-1:]
    odd = [k for pair in zip(near_half, far_half) for k in pair] + far_half[-1:]
    turns = [jnp.where(lax.rem(g, 2) == 0, k, l) for k, l in zip(even, odd)]

    def share_of(dest, c, part):
        col = pl.multiple_of(part * width + dest * share + c * LANES, LANES)
        return spec_ref.at[:, :, pl.ds(col, LANES)]

    def stage_copy(c, k, part):
        return pltpu.make_async_copy(share_of(partner(k), c, part), stage.at[c, k, part], stage_sem.at[c, k, part])

    def own_copy(c, part):
        return pltpu.make_async_copy(share_of(me, c, part), recv.at[c, me, part], own_sem.at[c, part])

    def spectra_copy(c, k):
        return pltpu.make_async_remote_copy(
            src_ref=stage.at[c, k],
            dst_ref=recv.at[c, me],
            send_sem=send_sem.at[c, k],
            recv_sem=recv_sem.at[c, me],
            device_id=(partner(k), g),
            device_id_type=MESH,
        )

    for c in range(chunks):
        for k in turns:
            for part in range(2):
                stage_copy(c, k, part).start()
        for part in range(2):
            own_copy(c, part).start()

    barrier = pltpu.get_barrier_semaphore()
    for t in range(1, n_sta):
        pl.semaphore_signal(
            barrier, inc=1, device_id=(lax.rem(me + t, n_sta), g), device_id_type=MESH
        )
    for t in range(1, n_win):
        pl.semaphore_signal(
            barrier, inc=1, device_id=(me, lax.rem(g + t, n_win)), device_id_type=MESH
        )
    lane = lax.broadcasted_iota(jnp.int32, (1, lab.shape[2]), 1)
    row = jnp.full((1, lab.shape[2]), -2, jnp.int32)
    for r in range(rounds):
        for j in range(stations):
            for i in range(stations):
                row = jnp.where(lane == (r * ROWS + j) * ROWS + i, bins_ref[r, i, j], row)
    lab[pl.ds(me, 1)] = row[None]

    sub = lax.broadcasted_iota(jnp.int32, (n_sta * CAP, LANES), 0)
    slot = jnp.full((n_sta * CAP, LANES), -1, jnp.int32)
    start = jnp.int32(0)
    for o in range(n_sta):
        held = count_ref[o]
        for k in range(CAP):
            chosen = order_ref[jnp.clip(start + k, 0, order_ref.shape[0] - 1)]
            slot = jnp.where(sub == o * CAP + k, jnp.where(k < held, chosen, -1), slot)
        start = start + held
    slots[...] = slot

    wide[...] = jnp.zeros_like(wide)
    pl.semaphore_wait(barrier, n_sta + n_win - 2)

    def label_copy(k):
        return pltpu.make_async_remote_copy(
            src_ref=lab.at[me],
            dst_ref=lab.at[me],
            send_sem=lab_send.at[k],
            recv_sem=lab_recv.at[me],
            device_id=(lax.rem(me + k, n_sta), g),
            device_id_type=MESH,
        )

    for k in range(1, n_sta):
        label_copy(k).start()

    for k in turns:
        for part in range(2):
            stage_copy(0, k, part).wait()
        spectra_copy(0, k).start()

    for c in range(1, chunks):
        for k in turns:
            for part in range(2):
                stage_copy(c, k, part).wait()
            spectra_copy(c, k).start()

    for k in range(1, n_sta):
        src = lax.rem(me - k + n_sta, n_sta)
        pltpu.make_async_remote_copy(
            src_ref=lab.at[src], dst_ref=lab.at[src], send_sem=lab_send.at[k],
            recv_sem=lab_recv.at[src], device_id=(src, g), device_id_type=MESH,
        ).wait_recv()

    def widen(c, p):
        for j in range(stations):
            x = recv[c, p, 0, j].astype(jnp.float32)
            y = recv[c, p, 1, j].astype(jnp.float32)
            for part, value in enumerate((x, y, x + y, x - y)):
                wide[p, part, pl.ds(j, windows, stride=ROWS), :] = value

    def arrive(c, src):
        @pl.when(src != me)
        def _():
            pltpu.make_async_remote_copy(
                src_ref=recv.at[c, src], dst_ref=recv.at[c, src],
                send_sem=send_sem.at[c, 0], recv_sem=recv_sem.at[c, src],
                device_id=(src, g), device_id_type=MESH,
            ).wait_recv()
            widen(c, src)

    def step(p, at_buffer):
        blocks = [lax.rem(p + r, n_sta) for r in range(rounds)]
        both = [[None] * stations for _ in range(rounds)]
        minus_re = [[None] * stations for _ in range(rounds)]
        minus_im = [[None] * stations for _ in range(rounds)]
        half = -(-stations // 2)
        for group in (range(half), range(half, stations)):
            for w in range(windows):
                at = pl.ds(w * ROWS, ROWS)
                mine = [[wide[b, part, at, :] for part in range(3)] for b in blocks]
                for j in group:
                    a, a_plus_b, a_minus_b = [
                        wide[p, part, pl.ds(w * ROWS + j, ROWS, stride=0), :] for part in (0, 2, 3)
                    ]
                    for r in range(rounds):
                        x, y, x_plus_y = mine[r]
                        terms = (a * x_plus_y, y * a_minus_b, x * a_plus_b)
                        for sums, term in zip((both, minus_re, minus_im), terms):
                            sums[r][j] = term if w == 0 else sums[r][j] + term
        re = [[u - v for u, v in zip(both[r], minus_re[r])] for r in range(rounds)]
        im = [[u - v for u, v in zip(both[r], minus_im[r])] for r in range(rounds)]
        blank = jnp.zeros((ROWS, LANES), jnp.float32)
        for r in range(rounds):
            at = pl.ds(r * ROWS * ROWS, ROWS * ROWS)
            pad = [blank] * (ROWS - stations)
            crossed[at_buffer, at, 0:LANES] = jnp.concatenate(re[r] + pad, axis=0).astype(jnp.bfloat16)
            crossed[at_buffer, at, LANES:] = jnp.concatenate(im[r] + pad, axis=0).astype(jnp.bfloat16)

    def binned(p, at_buffer):
        blocks = [lax.rem(p + r, n_sta) for r in range(rounds)]
        lanes = lax.broadcasted_iota(jnp.int32, (1, lab.shape[2]), 1)
        names = jnp.full((1, lab.shape[2]), -2, jnp.int32)
        for r in range(rounds):
            names = jnp.where(lanes // (ROWS * ROWS) == r, lab[blocks[r]], names)
        match = jnp.concatenate(
            [slots[...] == names[:, at:at + LANES] for at in range(0, lab.shape[2], LANES)], axis=1
        )
        match = jnp.where(match, 1.0, 0.0).astype(jnp.bfloat16)
        return jnp.dot(match, crossed[at_buffer], preferred_element_type=jnp.float32)

    def box_copies(c, k, part):
        o = partner(k)
        q = part * halves + me // per_out
        t = lax.rem(me, per_out)
        col = pl.multiple_of(t * share + c * LANES, LANES)
        src = outbox.at[c, part, o]
        dst = inbox.at[g, :, pl.ds(col, LANES)]

        def far():
            return pltpu.make_async_remote_copy(
                src_ref=src, dst_ref=dst, send_sem=box_send.at[c, part, k],
                recv_sem=box_recv.at[c, t, g], device_id=(o, q), device_id_type=MESH,
            )

        def near():
            return pltpu.make_async_copy(src, dst, box_recv.at[c, t, g])

        return far, near, q == g

    quarter = n_sta // 4
    place = lax.rem(me, 2 * quarter) // quarter * 2 + lax.rem(me, 2)
    low = me // (n_sta // 2) * (n_sta // 2)
    way = jnp.where(place == 3, -1, 1)
    first = low + jnp.where(place == 3, 1, jnp.where(place == 2, n_sta - 2, 0))

    def block_at(t):
        return lax.rem(first + way * t + 2 * n_sta, n_sta)

    def one_chunk(c, carry):
        for part in range(2):
            own_copy(c, part).wait()
        widen(c, me)
        for r in range(rounds - 1):
            arrive(c, lax.rem(block_at(0) + r + jnp.where(way < 0, 1, 0), n_sta))
        total[...] = jnp.zeros_like(total)
        crossed[...] = jnp.zeros_like(crossed)

        def one_step(t, carry):
            p = block_at(t)

            @pl.when(t <= n_sta - rounds)
            def _():
                arrive(c, lax.rem(p + jnp.where(way < 0, 0, rounds - 1), n_sta))

            now = lax.rem(t, 2)
            total[...] += binned(block_at(t - 1), 1 - now)
            step(p, now)
            return carry

        lax.fori_loop(0, n_sta, one_step, 0)
        total[...] += binned(block_at(n_sta - 1), (n_sta - 1) % 2)
        for part in range(2):
            for o in range(n_sta):
                outbox[c, part, o] = total[o * CAP:(o + 1) * CAP, part * LANES:(part + 1) * LANES]
        for part in range(2):
            for k in range(n_sta):
                far, near, is_me = box_copies(c, k, part)
                if k:
                    far().start()
                else:
                    pl.when(is_me)(lambda near=near: near().start())
                    pl.when(jnp.logical_not(is_me))(lambda far=far: far().start())
        return carry

    lax.fori_loop(0, chunks, one_chunk, 0)

    for c in range(chunks):
        for t in range(per_out):
            for s in range(n_win):
                dst = inbox.at[s, :, pl.ds(t * share + c * LANES, LANES)]
                pltpu.make_async_copy(dst, dst, box_recv.at[c, t, s]).wait()
    out_ref[...] = functools.reduce(jnp.add, [inbox[s] for s in range(n_win)])

    for c in range(chunks):
        for k in turns:
            spectra_copy(c, k).wait_send()
    for c in range(chunks):
        for part in range(2):
            for k in range(n_sta):
                far, near, is_me = box_copies(c, k, part)
                if k:
                    far().wait_send()
                else:
                    pl.when(jnp.logical_not(is_me))(lambda far=far: far().wait_send())
    for k in range(1, n_sta):
        label_copy(k).wait_send()


def by_frequency(spectra, pair_bins, owner_count, bin_order):
    n_sta, n_win = lax.axis_size("sta"), lax.axis_size("win")
    windows, stations, columns = spectra.shape
    rounds = pair_bins.shape[1]
    width = columns // 2
    share = width // n_sta
    chunks = share // LANES
    out_cols = columns // n_win
    per_out = out_cols // share
    depth = -(-rounds * ROWS * ROWS // LANES) * LANES
    sizes = (n_sta, n_win, chunks, windows, stations, rounds, width)
    dma = pltpu.SemaphoreType.DMA
    sums = pl.pallas_call(
        functools.partial(kernel, sizes),
        out_shape=jax.ShapeDtypeStruct((CAP, out_cols), jnp.float32),
        in_specs=[
            pl.BlockSpec(memory_space=pl.ANY),
            pl.BlockSpec(memory_space=pltpu.SMEM),
            pl.BlockSpec(memory_space=pltpu.SMEM),
            pl.BlockSpec(memory_space=pltpu.SMEM),
        ],
        out_specs=pl.BlockSpec(memory_space=pltpu.VMEM),
        scratch_shapes=[
            pltpu.VMEM((chunks, n_sta, 2, stations, windows, LANES), spectra.dtype),
            pltpu.VMEM((chunks, n_sta, 2, stations, windows, LANES), spectra.dtype),
            pltpu.VMEM((n_sta, 4, windows * ROWS, LANES), jnp.float32),
            pltpu.VMEM((n_sta, 1, depth), jnp.int32),
            pltpu.VMEM((n_sta * CAP, LANES), jnp.int32),
            pltpu.VMEM((2, depth, 2 * LANES), jnp.bfloat16),
            pltpu.VMEM((n_sta * CAP, 2 * LANES), jnp.float32),
            pltpu.VMEM((chunks, 2, n_sta, CAP, LANES), jnp.float32),
            pltpu.VMEM((n_win, CAP, out_cols), jnp.float32),
            dma((chunks, n_sta, 2)),
            dma((chunks, n_sta)),
            dma((chunks, n_sta)),
            dma((chunks, 2)),
            dma((n_sta,)),
            dma((n_sta,)),
            dma((chunks, 2, n_sta)),
            dma((chunks, per_out, n_win)),
        ],
        compiler_params=pltpu.CompilerParams(
            collective_id=0, has_side_effects=True, vmem_limit_bytes=56 * 1024 * 1024
        ),
        cost_estimate=pl.CostEstimate(
            flops=8 * width * windows * rounds * stations * stations,
            bytes_accessed=2 * spectra.size, transcendentals=0,
        ),
    )(jnp.transpose(spectra, (1, 0, 2)), jnp.transpose(pair_bins, (1, 0, 2)), owner_count, bin_order)
    return sums * jnp.float32(1.0 / (windows * n_win))


def on_device(spectra, pair_bins, owner_count, bin_order):
    n_sta, n_win = lax.axis_size("sta"), lax.axis_size("win")
    width = spectra.shape[2] // 2
    share, out_cols = width // n_sta, 2 * width // n_win
    fits = (
        width % (n_sta * LANES) == 0 and out_cols % share == 0 and width % out_cols == 0
        and spectra.shape[1] <= ROWS and pair_bins.shape[1] <= n_sta - 1
    )
    plan = by_frequency if fits else by_blocks
    return plan(spectra, pair_bins, owner_count, bin_order)


def solution(mesh):
    return jax.shard_map(
        on_device,
        mesh=mesh,
        in_specs=(P("win", "sta", None), P("sta", None, None), P(), P()),
        out_specs=P("sta", "win"),
        check_vma=False,
    )
```

```python
import functools
import jax
import jax.numpy as jnp
from jax import lax
from jax.experimental import pallas as pl
from jax.experimental.pallas import tpu as pltpu
from jax.sharding import PartitionSpec as P

CAP = 4
LANES = 128
ROWS = 8
MESH = pl.DeviceIdType.MESH


def passed_along(value, axis, steps):
    count = lax.axis_size(axis)
    pairs = [(source, (source + steps) % count) for source in range(count)]
    return lax.ppermute(value, axis, pairs)


def cross_pairs(own, other):
    width = own.shape[-1] // 2
    own_re, own_im = (own[..., :width], own[..., width:])
    other_re, other_im = (other[..., :width], other[..., width:])
    form = "wsf,wtf->stf"
    real = jnp.einsum(form, own_re, other_re, preferred_element_type=jnp.float32) + jnp.einsum(
        form, own_im, other_im, preferred_element_type=jnp.float32
    )
    imag = jnp.einsum(form, own_im, other_re, preferred_element_type=jnp.float32) - jnp.einsum(
        form, own_re, other_im, preferred_element_type=jnp.float32
    )
    joined = jnp.concatenate([real, imag], axis=-1).astype(jnp.bfloat16)
    return joined.reshape(-1, joined.shape[-1])


def by_blocks(spectra, pair_bins, owner_count, bin_order):
    rounds = pair_bins.shape[1]
    blocks = [spectra]
    for offset in range(1, rounds):
        blocks.append(passed_along(spectra, "sta", offset))
    crossed = jnp.concatenate([cross_pairs(spectra, other) for other in blocks], axis=0)
    labels = jnp.transpose(pair_bins, (1, 0, 2)).reshape(-1)
    bin_total = bin_order.shape[0]
    starts = jnp.cumsum(owner_count) - owner_count
    ranks = jnp.arange(CAP, dtype=jnp.int32)
    positions = jnp.clip(starts[:, None] + ranks[None, :], 0, bin_total - 1)
    valid = ranks[None, :] < owner_count[:, None]
    chosen = jnp.take(bin_order, positions)
    slot_bin = jnp.where(valid, chosen, -1).reshape(-1)
    window_total = spectra.shape[0] * lax.axis_size("win")
    matches = (slot_bin[:, None] == labels[None, :]).astype(jnp.bfloat16)
    partial_sums = jnp.dot(matches, crossed, preferred_element_type=jnp.float32)
    spread = lax.psum_scatter(partial_sums, "win", scatter_dimension=1, tiled=True)
    stacks = lax.psum_scatter(spread, "sta", scatter_dimension=0, tiled=True)
    return stacks * jnp.float32(1.0 / window_total)


def kernel(
    sizes, spec_ref, bins_ref, count_ref, order_ref, out_ref,
    stage, recv, wide, lab, slots, crossed, total, outbox, inbox,
    stage_sem, send_sem, recv_sem, own_sem, lab_send, lab_recv, box_send, box_recv,
):
    n_sta, n_win, chunks, windows, stations, rounds, width = sizes
    share = width // n_sta
    out_cols = out_ref.shape[1]
    per_out = out_cols // share
    halves = width // out_cols
    me = lax.axis_index("sta")
    g = lax.axis_index("win")

    def partner(k):
        if n_sta & (n_sta - 1):
            return lax.rem(me + k, n_sta)
        digits, bit = me, 1
        while bit < n_sta:
            if k & bit:
                digits = digits + bit - 2 * bit * lax.rem(digits // bit, 2)
            bit *= 2
        return digits

    far_half = list(range(n_sta // 2, n_sta))
    near_half = list(range(1, n_sta // 2)) + [None]
    turns = [k for pair in zip(far_half, near_half) for k in pair if k is not None]

    def share_of(dest, c, part):
        col = pl.multiple_of(part * width + dest * share + c * LANES, LANES)
        return spec_ref.at[:, :, pl.ds(col, LANES)]

    def stage_copy(c, k, part):
        return pltpu.make_async_copy(share_of(partner(k), c, part), stage.at[c, k, part], stage_sem.at[c, k, part])

    def own_copy(c, part):
        return pltpu.make_async_copy(share_of(me, c, part), recv.at[c, me, part], own_sem.at[c, part])

    def spectra_copy(c, k):
        return pltpu.make_async_remote_copy(
            src_ref=stage.at[c, k],
            dst_ref=recv.at[c, me],
            send_sem=send_sem.at[c, k],
            recv_sem=recv_sem.at[c, me],
            device_id=(partner(k), g),
            device_id_type=MESH,
        )

    barrier = pltpu.get_barrier_semaphore()
    for t in range(1, n_sta):
        pl.semaphore_signal(
            barrier, inc=1, device_id=(lax.rem(me + t, n_sta), g), device_id_type=MESH
        )
    for t in range(1, n_win):
        pl.semaphore_signal(
            barrier, inc=1, device_id=(me, lax.rem(g + t, n_win)), device_id_type=MESH
        )
    def stage_chunk(c):
        for k in turns:
            for part in range(2):
                stage_copy(c, k, part).start()

    stage_chunk(0)
    pl.semaphore_wait(barrier, n_sta + n_win - 2)

    for k in turns:
        for part in range(2):
            stage_copy(0, k, part).wait()
        spectra_copy(0, k).start()

    for c in range(1, chunks):
        stage_chunk(c)
    for c in range(chunks):
        for part in range(2):
            own_copy(c, part).start()

    lane = lax.broadcasted_iota(jnp.int32, (1, lab.shape[2]), 1)
    row = jnp.full((1, lab.shape[2]), -2, jnp.int32)
    for r in range(rounds):
        for j in range(stations):
            for i in range(stations):
                row = jnp.where(lane == (r * ROWS + j) * ROWS + i, bins_ref[r, i, j], row)
    lab[pl.ds(me, 1)] = row[None]

    def label_copy(k):
        return pltpu.make_async_remote_copy(
            src_ref=lab.at[me],
            dst_ref=lab.at[me],
            send_sem=lab_send.at[k],
            recv_sem=lab_recv.at[me],
            device_id=(lax.rem(me + k, n_sta), g),
            device_id_type=MESH,
        )

    for k in range(1, n_sta):
        label_copy(k).start()

    for c in range(1, chunks):
        for k in turns:
            for part in range(2):
                stage_copy(c, k, part).wait()
            spectra_copy(c, k).start()

    sub = lax.broadcasted_iota(jnp.int32, (n_sta * CAP, LANES), 0)
    slot = jnp.full((n_sta * CAP, LANES), -1, jnp.int32)
    start = jnp.int32(0)
    for o in range(n_sta):
        held = count_ref[o]
        for k in range(CAP):
            chosen = order_ref[jnp.clip(start + k, 0, order_ref.shape[0] - 1)]
            slot = jnp.where(sub == o * CAP + k, jnp.where(k < held, chosen, -1), slot)
        start = start + held
    slots[...] = slot

    wide[...] = jnp.zeros_like(wide)
    for k in range(1, n_sta):
        src = lax.rem(me - k + n_sta, n_sta)
        pltpu.make_async_remote_copy(
            src_ref=lab.at[src], dst_ref=lab.at[src], send_sem=lab_send.at[k],
            recv_sem=lab_recv.at[src], device_id=(src, g), device_id_type=MESH,
        ).wait_recv()

    def widen(c, p):
        for j in range(stations):
            x = recv[c, p, 0, j].astype(jnp.float32)
            y = recv[c, p, 1, j].astype(jnp.float32)
            for part, value in enumerate((x, y, x + y, x - y)):
                wide[p, part, pl.ds(j, windows, stride=ROWS), :] = value

    def arrive(c, src):
        @pl.when(src != me)
        def _():
            pltpu.make_async_remote_copy(
                src_ref=recv.at[c, src], dst_ref=recv.at[c, src],
                send_sem=send_sem.at[c, 0], recv_sem=recv_sem.at[c, src],
                device_id=(src, g), device_id_type=MESH,
            ).wait_recv()
            widen(c, src)

    def step(p, at_buffer):
        blocks = [lax.rem(p + r, n_sta) for r in range(rounds)]
        both = [[None] * stations for _ in range(rounds)]
        minus_re = [[None] * stations for _ in range(rounds)]
        minus_im = [[None] * stations for _ in range(rounds)]
        half = -(-stations // 2)
        for group in (range(half), range(half, stations)):
            for w in range(windows):
                at = pl.ds(w * ROWS, ROWS)
                mine = [[wide[b, part, at, :] for part in range(3)] for b in blocks]
                for j in group:
                    a, a_plus_b, a_minus_b = [
                        wide[p, part, pl.ds(w * ROWS + j, ROWS, stride=0), :] for part in (0, 2, 3)
                    ]
                    for r in range(rounds):
                        x, y, x_plus_y = mine[r]
                        terms = (a * x_plus_y, y * a_minus_b, x * a_plus_b)
                        for sums, term in zip((both, minus_re, minus_im), terms):
                            sums[r][j] = term if w == 0 else sums[r][j] + term
        re = [[u - v for u, v in zip(both[r], minus_re[r])] for r in range(rounds)]
        im = [[u - v for u, v in zip(both[r], minus_im[r])] for r in range(rounds)]
        blank = jnp.zeros((ROWS, LANES), jnp.float32)
        for r in range(rounds):
            at = pl.ds(r * ROWS * ROWS, ROWS * ROWS)
            pad = [blank] * (ROWS - stations)
            crossed[at_buffer, at, 0:LANES] = jnp.concatenate(re[r] + pad, axis=0).astype(jnp.bfloat16)
            crossed[at_buffer, at, LANES:] = jnp.concatenate(im[r] + pad, axis=0).astype(jnp.bfloat16)

    def binned(p, at_buffer):
        blocks = [lax.rem(p + r, n_sta) for r in range(rounds)]
        lanes = lax.broadcasted_iota(jnp.int32, (1, lab.shape[2]), 1)
        names = jnp.full((1, lab.shape[2]), -2, jnp.int32)
        for r in range(rounds):
            names = jnp.where(lanes // (ROWS * ROWS) == r, lab[blocks[r]], names)
        match = jnp.concatenate(
            [slots[...] == names[:, at:at + LANES] for at in range(0, lab.shape[2], LANES)], axis=1
        )
        match = jnp.where(match, 1.0, 0.0).astype(jnp.bfloat16)
        return jnp.dot(match, crossed[at_buffer], preferred_element_type=jnp.float32)

    def box_copies(c, k, part):
        o = partner(k)
        q = part * halves + me // per_out
        t = lax.rem(me, per_out)
        col = pl.multiple_of(t * share + c * LANES, LANES)
        src = outbox.at[c, part, o]
        dst = inbox.at[g, :, pl.ds(col, LANES)]

        def far():
            return pltpu.make_async_remote_copy(
                src_ref=src, dst_ref=dst, send_sem=box_send.at[c, part, k],
                recv_sem=box_recv.at[c, t, g], device_id=(o, q), device_id_type=MESH,
            )

        def near():
            return pltpu.make_async_copy(src, dst, box_recv.at[c, t, g])

        return far, near, q == g

    quarter = n_sta // 4
    place = lax.rem(me, 2 * quarter) // quarter * 2 + lax.rem(me, 2)
    low = me // (n_sta // 2) * (n_sta // 2)
    way = jnp.where(place == 3, -1, 1)
    first = low + jnp.where(place == 3, 1, jnp.where(place == 2, n_sta - 2, 0))

    def block_at(t):
        return lax.rem(first + way * t + 2 * n_sta, n_sta)

    def one_chunk(c, carry):
        for part in range(2):
            own_copy(c, part).wait()
        widen(c, me)
        for r in range(rounds - 1):
            arrive(c, lax.rem(block_at(0) + r + jnp.where(way < 0, 1, 0), n_sta))
        total[...] = jnp.zeros_like(total)
        crossed[...] = jnp.zeros_like(crossed)

        def one_step(t, carry):
            p = block_at(t)

            @pl.when(t <= n_sta - rounds)
            def _():
                arrive(c, lax.rem(p + jnp.where(way < 0, 0, rounds - 1), n_sta))

            now = lax.rem(t, 2)
            total[...] += binned(block_at(t - 1), 1 - now)
            step(p, now)
            return carry

        lax.fori_loop(0, n_sta, one_step, 0)
        total[...] += binned(block_at(n_sta - 1), (n_sta - 1) % 2)
        for part in range(2):
            for o in range(n_sta):
                outbox[c, part, o] = total[o * CAP:(o + 1) * CAP, part * LANES:(part + 1) * LANES]
        for part in range(2):
            for k in range(n_sta):
                far, near, is_me = box_copies(c, k, part)
                if k:
                    far().start()
                else:
                    pl.when(is_me)(lambda near=near: near().start())
                    pl.when(jnp.logical_not(is_me))(lambda far=far: far().start())
        return carry

    lax.fori_loop(0, chunks, one_chunk, 0)

    for c in range(chunks):
        for t in range(per_out):
            for s in range(n_win):
                dst = inbox.at[s, :, pl.ds(t * share + c * LANES, LANES)]
                pltpu.make_async_copy(dst, dst, box_recv.at[c, t, s]).wait()
    out_ref[...] = functools.reduce(jnp.add, [inbox[s] for s in range(n_win)])

    for c in range(chunks):
        for k in turns:
            spectra_copy(c, k).wait_send()
    for c in range(chunks):
        for part in range(2):
            for k in range(n_sta):
                far, near, is_me = box_copies(c, k, part)
                if k:
                    far().wait_send()
                else:
                    pl.when(jnp.logical_not(is_me))(lambda far=far: far().wait_send())
    for k in range(1, n_sta):
        label_copy(k).wait_send()


def by_frequency(spectra, pair_bins, owner_count, bin_order):
    n_sta, n_win = lax.axis_size("sta"), lax.axis_size("win")
    windows, stations, columns = spectra.shape
    rounds = pair_bins.shape[1]
    width = columns // 2
    share = width // n_sta
    chunks = share // LANES
    out_cols = columns // n_win
    per_out = out_cols // share
    depth = -(-rounds * ROWS * ROWS // LANES) * LANES
    sizes = (n_sta, n_win, chunks, windows, stations, rounds, width)
    dma = pltpu.SemaphoreType.DMA
    sums = pl.pallas_call(
        functools.partial(kernel, sizes),
        out_shape=jax.ShapeDtypeStruct((CAP, out_cols), jnp.float32),
        in_specs=[
            pl.BlockSpec(memory_space=pl.ANY),
            pl.BlockSpec(memory_space=pltpu.SMEM),
            pl.BlockSpec(memory_space=pltpu.SMEM),
            pl.BlockSpec(memory_space=pltpu.SMEM),
        ],
        out_specs=pl.BlockSpec(memory_space=pltpu.VMEM),
        scratch_shapes=[
            pltpu.VMEM((chunks, n_sta, 2, stations, windows, LANES), spectra.dtype),
            pltpu.VMEM((chunks, n_sta, 2, stations, windows, LANES), spectra.dtype),
            pltpu.VMEM((n_sta, 4, windows * ROWS, LANES), jnp.float32),
            pltpu.VMEM((n_sta, 1, depth), jnp.int32),
            pltpu.VMEM((n_sta * CAP, LANES), jnp.int32),
            pltpu.VMEM((2, depth, 2 * LANES), jnp.bfloat16),
            pltpu.VMEM((n_sta * CAP, 2 * LANES), jnp.float32),
            pltpu.VMEM((chunks, 2, n_sta, CAP, LANES), jnp.float32),
            pltpu.VMEM((n_win, CAP, out_cols), jnp.float32),
            dma((chunks, n_sta, 2)),
            dma((chunks, n_sta)),
            dma((chunks, n_sta)),
            dma((chunks, 2)),
            dma((n_sta,)),
            dma((n_sta,)),
            dma((chunks, 2, n_sta)),
            dma((chunks, per_out, n_win)),
        ],
        compiler_params=pltpu.CompilerParams(
            collective_id=0, has_side_effects=True, vmem_limit_bytes=56 * 1024 * 1024
        ),
        cost_estimate=pl.CostEstimate(
            flops=8 * width * windows * rounds * stations * stations,
            bytes_accessed=2 * spectra.size, transcendentals=0,
        ),
    )(jnp.transpose(spectra, (1, 0, 2)), jnp.transpose(pair_bins, (1, 0, 2)), owner_count, bin_order)
    return sums * jnp.float32(1.0 / (windows * n_win))


def on_device(spectra, pair_bins, owner_count, bin_order):
    n_sta, n_win = lax.axis_size("sta"), lax.axis_size("win")
    width = spectra.shape[2] // 2
    share, out_cols = width // n_sta, 2 * width // n_win
    fits = (
        width % (n_sta * LANES) == 0 and out_cols % share == 0 and width % out_cols == 0
        and spectra.shape[1] <= ROWS and pair_bins.shape[1] <= n_sta - 1
    )
    plan = by_frequency if fits else by_blocks
    return plan(spectra, pair_bins, owner_count, bin_order)


def solution(mesh):
    return jax.shard_map(
        on_device,
        mesh=mesh,
        in_specs=(P("win", "sta", None), P("sta", None, None), P(), P()),
        out_specs=P("sta", "win"),
        check_vma=False,
    )
```

```python
import functools
import jax
import jax.numpy as jnp
from jax import lax
from jax.experimental import pallas as pl
from jax.experimental.pallas import tpu as pltpu
from jax.sharding import PartitionSpec as P

CAP = 4
LANES = 128
ROWS = 8
MESH = pl.DeviceIdType.MESH


def passed_along(value, axis, steps):
    count = lax.axis_size(axis)
    pairs = [(source, (source + steps) % count) for source in range(count)]
    return lax.ppermute(value, axis, pairs)


def cross_pairs(own, other):
    width = own.shape[-1] // 2
    own_re, own_im = (own[..., :width], own[..., width:])
    other_re, other_im = (other[..., :width], other[..., width:])
    form = "wsf,wtf->stf"
    real = jnp.einsum(form, own_re, other_re, preferred_element_type=jnp.float32) + jnp.einsum(
        form, own_im, other_im, preferred_element_type=jnp.float32
    )
    imag = jnp.einsum(form, own_im, other_re, preferred_element_type=jnp.float32) - jnp.einsum(
        form, own_re, other_im, preferred_element_type=jnp.float32
    )
    joined = jnp.concatenate([real, imag], axis=-1).astype(jnp.bfloat16)
    return joined.reshape(-1, joined.shape[-1])


def by_blocks(spectra, pair_bins, owner_count, bin_order):
    rounds = pair_bins.shape[1]
    blocks = [spectra]
    for offset in range(1, rounds):
        blocks.append(passed_along(spectra, "sta", offset))
    crossed = jnp.concatenate([cross_pairs(spectra, other) for other in blocks], axis=0)
    labels = jnp.transpose(pair_bins, (1, 0, 2)).reshape(-1)
    bin_total = bin_order.shape[0]
    starts = jnp.cumsum(owner_count) - owner_count
    ranks = jnp.arange(CAP, dtype=jnp.int32)
    positions = jnp.clip(starts[:, None] + ranks[None, :], 0, bin_total - 1)
    valid = ranks[None, :] < owner_count[:, None]
    chosen = jnp.take(bin_order, positions)
    slot_bin = jnp.where(valid, chosen, -1).reshape(-1)
    window_total = spectra.shape[0] * lax.axis_size("win")
    matches = (slot_bin[:, None] == labels[None, :]).astype(jnp.bfloat16)
    partial_sums = jnp.dot(matches, crossed, preferred_element_type=jnp.float32)
    spread = lax.psum_scatter(partial_sums, "win", scatter_dimension=1, tiled=True)
    stacks = lax.psum_scatter(spread, "sta", scatter_dimension=0, tiled=True)
    return stacks * jnp.float32(1.0 / window_total)


def kernel(
    sizes, spec_ref, bins_ref, count_ref, order_ref, out_ref,
    stage, recv, wide, lab, slots, crossed, total, outbox, inbox,
    stage_sem, send_sem, recv_sem, own_sem, lab_send, lab_recv, box_send, box_recv,
):
    n_sta, n_win, chunks, windows, stations, rounds, width = sizes
    share = width // n_sta
    out_cols = out_ref.shape[1]
    per_out = out_cols // share
    halves = width // out_cols
    me = lax.axis_index("sta")
    g = lax.axis_index("win")

    def partner(k):
        if n_sta & (n_sta - 1):
            return lax.rem(me + k, n_sta)
        digits, bit = me, 1
        while bit < n_sta:
            if k & bit:
                digits = digits + bit - 2 * bit * lax.rem(digits // bit, 2)
            bit *= 2
        return digits

    far_half = list(range(n_sta // 2, n_sta))
    near_half = list(range(1, n_sta // 2)) + [None]
    turns = [k for pair in zip(far_half, near_half) for k in pair if k is not None]

    def share_of(dest, c, part):
        col = pl.multiple_of(part * width + dest * share + c * LANES, LANES)
        return spec_ref.at[:, :, pl.ds(col, LANES)]

    def stage_copy(c, k, part):
        return pltpu.make_async_copy(share_of(partner(k), c, part), stage.at[c, k, part], stage_sem.at[c, k, part])

    def own_copy(c, part):
        return pltpu.make_async_copy(share_of(me, c, part), recv.at[c, me, part], own_sem.at[c, part])

    def spectra_copy(c, k):
        return pltpu.make_async_remote_copy(
            src_ref=stage.at[c, k],
            dst_ref=recv.at[c, me],
            send_sem=send_sem.at[c, k],
            recv_sem=recv_sem.at[c, me],
            device_id=(partner(k), g),
            device_id_type=MESH,
        )

    for c in range(chunks):
        for k in turns:
            for part in range(2):
                stage_copy(c, k, part).start()
        for part in range(2):
            own_copy(c, part).start()

    barrier = pltpu.get_barrier_semaphore()
    for t in range(1, n_sta):
        pl.semaphore_signal(
            barrier, inc=1, device_id=(lax.rem(me + t, n_sta), g), device_id_type=MESH
        )
    for t in range(1, n_win):
        pl.semaphore_signal(
            barrier, inc=1, device_id=(me, lax.rem(g + t, n_win)), device_id_type=MESH
        )
    lane = lax.broadcasted_iota(jnp.int32, (1, lab.shape[2]), 1)
    row = jnp.full((1, lab.shape[2]), -2, jnp.int32)
    for r in range(rounds):
        for j in range(stations):
            for i in range(stations):
                row = jnp.where(lane == (r * ROWS + j) * ROWS + i, bins_ref[r, i, j], row)
    lab[pl.ds(me, 1)] = row[None]

    pl.semaphore_wait(barrier, n_sta + n_win - 2)

    def label_copy(k):
        return pltpu.make_async_remote_copy(
            src_ref=lab.at[me],
            dst_ref=lab.at[me],
            send_sem=lab_send.at[k],
            recv_sem=lab_recv.at[me],
            device_id=(lax.rem(me + k, n_sta), g),
            device_id_type=MESH,
        )

    for k in range(1, n_sta):
        label_copy(k).start()

    for k in turns:
        for part in range(2):
            stage_copy(0, k, part).wait()
        spectra_copy(0, k).start()

    for c in range(1, chunks):
        for k in turns:
            for part in range(2):
                stage_copy(c, k, part).wait()
            spectra_copy(c, k).start()

    sub = lax.broadcasted_iota(jnp.int32, (n_sta * CAP, LANES), 0)
    slot = jnp.full((n_sta * CAP, LANES), -1, jnp.int32)
    start = jnp.int32(0)
    for o in range(n_sta):
        held = count_ref[o]
        for k in range(CAP):
            chosen = order_ref[jnp.clip(start + k, 0, order_ref.shape[0] - 1)]
            slot = jnp.where(sub == o * CAP + k, jnp.where(k < held, chosen, -1), slot)
        start = start + held
    slots[...] = slot

    wide[...] = jnp.zeros_like(wide)
    for k in range(1, n_sta):
        src = lax.rem(me - k + n_sta, n_sta)
        pltpu.make_async_remote_copy(
            src_ref=lab.at[src], dst_ref=lab.at[src], send_sem=lab_send.at[k],
            recv_sem=lab_recv.at[src], device_id=(src, g), device_id_type=MESH,
        ).wait_recv()

    def widen(c, p):
        for j in range(stations):
            x = recv[c, p, 0, j].astype(jnp.float32)
            y = recv[c, p, 1, j].astype(jnp.float32)
            for part, value in enumerate((x, y, x + y, x - y)):
                wide[p, part, pl.ds(j, windows, stride=ROWS), :] = value

    def arrive(c, src):
        @pl.when(src != me)
        def _():
            pltpu.make_async_remote_copy(
                src_ref=recv.at[c, src], dst_ref=recv.at[c, src],
                send_sem=send_sem.at[c, 0], recv_sem=recv_sem.at[c, src],
                device_id=(src, g), device_id_type=MESH,
            ).wait_recv()
            widen(c, src)

    def step(p, at_buffer):
        blocks = [lax.rem(p + r, n_sta) for r in range(rounds)]
        both = [[None] * stations for _ in range(rounds)]
        minus_re = [[None] * stations for _ in range(rounds)]
        minus_im = [[None] * stations for _ in range(rounds)]
        half = -(-stations // 2)
        for group in (range(half), range(half, stations)):
            for w in range(windows):
                at = pl.ds(w * ROWS, ROWS)
                mine = [[wide[b, part, at, :] for part in range(3)] for b in blocks]
                for j in group:
                    a, a_plus_b, a_minus_b = [
                        wide[p, part, pl.ds(w * ROWS + j, ROWS, stride=0), :] for part in (0, 2, 3)
                    ]
                    for r in range(rounds):
                        x, y, x_plus_y = mine[r]
                        terms = (a * x_plus_y, y * a_minus_b, x * a_plus_b)
                        for sums, term in zip((both, minus_re, minus_im), terms):
                            sums[r][j] = term if w == 0 else sums[r][j] + term
        re = [[u - v for u, v in zip(both[r], minus_re[r])] for r in range(rounds)]
        im = [[u - v for u, v in zip(both[r], minus_im[r])] for r in range(rounds)]
        blank = jnp.zeros((ROWS, LANES), jnp.float32)
        for r in range(rounds):
            at = pl.ds(r * ROWS * ROWS, ROWS * ROWS)
            pad = [blank] * (ROWS - stations)
            crossed[at_buffer, at, 0:LANES] = jnp.concatenate(re[r] + pad, axis=0).astype(jnp.bfloat16)
            crossed[at_buffer, at, LANES:] = jnp.concatenate(im[r] + pad, axis=0).astype(jnp.bfloat16)

    def binned(p, at_buffer):
        blocks = [lax.rem(p + r, n_sta) for r in range(rounds)]
        lanes = lax.broadcasted_iota(jnp.int32, (1, lab.shape[2]), 1)
        names = jnp.full((1, lab.shape[2]), -2, jnp.int32)
        for r in range(rounds):
            names = jnp.where(lanes // (ROWS * ROWS) == r, lab[blocks[r]], names)
        match = jnp.concatenate(
            [slots[...] == names[:, at:at + LANES] for at in range(0, lab.shape[2], LANES)], axis=1
        )
        match = jnp.where(match, 1.0, 0.0).astype(jnp.bfloat16)
        return jnp.dot(match, crossed[at_buffer], preferred_element_type=jnp.float32)

    def box_copies(c, k, part):
        o = partner(k)
        q = part * halves + me // per_out
        t = lax.rem(me, per_out)
        col = pl.multiple_of(t * share + c * LANES, LANES)
        src = outbox.at[c, part, o]
        dst = inbox.at[g, :, pl.ds(col, LANES)]

        def far():
            return pltpu.make_async_remote_copy(
                src_ref=src, dst_ref=dst, send_sem=box_send.at[c, part, k],
                recv_sem=box_recv.at[c, t, g], device_id=(o, q), device_id_type=MESH,
            )

        def near():
            return pltpu.make_async_copy(src, dst, box_recv.at[c, t, g])

        return far, near, q == g

    quarter = n_sta // 4
    place = lax.rem(me, 2 * quarter) // quarter * 2 + lax.rem(me, 2)
    low = me // (n_sta // 2) * (n_sta // 2)
    way = jnp.where(place == 3, -1, 1)
    first = low + jnp.where(place == 3, 1, jnp.where(place == 2, n_sta - 2, 0))

    def block_at(t):
        return lax.rem(first + way * t + 2 * n_sta, n_sta)

    def one_chunk(c, carry):
        for part in range(2):
            own_copy(c, part).wait()
        widen(c, me)
        for r in range(rounds - 1):
            arrive(c, lax.rem(block_at(0) + r + jnp.where(way < 0, 1, 0), n_sta))
        total[...] = jnp.zeros_like(total)
        crossed[...] = jnp.zeros_like(crossed)

        def one_step(t, carry):
            p = block_at(t)

            @pl.when(t <= n_sta - rounds)
            def _():
                arrive(c, lax.rem(p + jnp.where(way < 0, 0, rounds - 1), n_sta))

            now = lax.rem(t, 2)
            total[...] += binned(block_at(t - 1), 1 - now)
            step(p, now)
            return carry

        lax.fori_loop(0, n_sta, one_step, 0)
        total[...] += binned(block_at(n_sta - 1), (n_sta - 1) % 2)
        for part in range(2):
            for o in range(n_sta):
                outbox[c, part, o] = total[o * CAP:(o + 1) * CAP, part * LANES:(part + 1) * LANES]
        for part in range(2):
            for k in range(n_sta):
                far, near, is_me = box_copies(c, k, part)
                if k:
                    far().start()
                else:
                    pl.when(is_me)(lambda near=near: near().start())
                    pl.when(jnp.logical_not(is_me))(lambda far=far: far().start())
        return carry

    lax.fori_loop(0, chunks, one_chunk, 0)

    for c in range(chunks):
        for t in range(per_out):
            for s in range(n_win):
                dst = inbox.at[s, :, pl.ds(t * share + c * LANES, LANES)]
                pltpu.make_async_copy(dst, dst, box_recv.at[c, t, s]).wait()
    out_ref[...] = functools.reduce(jnp.add, [inbox[s] for s in range(n_win)])

    for c in range(chunks):
        for k in turns:
            spectra_copy(c, k).wait_send()
    for c in range(chunks):
        for part in range(2):
            for k in range(n_sta):
                far, near, is_me = box_copies(c, k, part)
                if k:
                    far().wait_send()
                else:
                    pl.when(jnp.logical_not(is_me))(lambda far=far: far().wait_send())
    for k in range(1, n_sta):
        label_copy(k).wait_send()


def by_frequency(spectra, pair_bins, owner_count, bin_order):
    n_sta, n_win = lax.axis_size("sta"), lax.axis_size("win")
    windows, stations, columns = spectra.shape
    rounds = pair_bins.shape[1]
    width = columns // 2
    share = width // n_sta
    chunks = share // LANES
    out_cols = columns // n_win
    per_out = out_cols // share
    depth = -(-rounds * ROWS * ROWS // LANES) * LANES
    sizes = (n_sta, n_win, chunks, windows, stations, rounds, width)
    dma = pltpu.SemaphoreType.DMA
    sums = pl.pallas_call(
        functools.partial(kernel, sizes),
        out_shape=jax.ShapeDtypeStruct((CAP, out_cols), jnp.float32),
        in_specs=[
            pl.BlockSpec(memory_space=pl.ANY),
            pl.BlockSpec(memory_space=pltpu.SMEM),
            pl.BlockSpec(memory_space=pltpu.SMEM),
            pl.BlockSpec(memory_space=pltpu.SMEM),
        ],
        out_specs=pl.BlockSpec(memory_space=pltpu.VMEM),
        scratch_shapes=[
            pltpu.VMEM((chunks, n_sta, 2, stations, windows, LANES), spectra.dtype),
            pltpu.VMEM((chunks, n_sta, 2, stations, windows, LANES), spectra.dtype),
            pltpu.VMEM((n_sta, 4, windows * ROWS, LANES), jnp.float32),
            pltpu.VMEM((n_sta, 1, depth), jnp.int32),
            pltpu.VMEM((n_sta * CAP, LANES), jnp.int32),
            pltpu.VMEM((2, depth, 2 * LANES), jnp.bfloat16),
            pltpu.VMEM((n_sta * CAP, 2 * LANES), jnp.float32),
            pltpu.VMEM((chunks, 2, n_sta, CAP, LANES), jnp.float32),
            pltpu.VMEM((n_win, CAP, out_cols), jnp.float32),
            dma((chunks, n_sta, 2)),
            dma((chunks, n_sta)),
            dma((chunks, n_sta)),
            dma((chunks, 2)),
            dma((n_sta,)),
            dma((n_sta,)),
            dma((chunks, 2, n_sta)),
            dma((chunks, per_out, n_win)),
        ],
        compiler_params=pltpu.CompilerParams(
            collective_id=0, has_side_effects=True, vmem_limit_bytes=56 * 1024 * 1024
        ),
        cost_estimate=pl.CostEstimate(
            flops=8 * width * windows * rounds * stations * stations,
            bytes_accessed=2 * spectra.size, transcendentals=0,
        ),
    )(jnp.transpose(spectra, (1, 0, 2)), jnp.transpose(pair_bins, (1, 0, 2)), owner_count, bin_order)
    return sums * jnp.float32(1.0 / (windows * n_win))


def on_device(spectra, pair_bins, owner_count, bin_order):
    n_sta, n_win = lax.axis_size("sta"), lax.axis_size("win")
    width = spectra.shape[2] // 2
    share, out_cols = width // n_sta, 2 * width // n_win
    fits = (
        width % (n_sta * LANES) == 0 and out_cols % share == 0 and width % out_cols == 0
        and spectra.shape[1] <= ROWS and pair_bins.shape[1] <= n_sta - 1
    )
    plan = by_frequency if fits else by_blocks
    return plan(spectra, pair_bins, owner_count, bin_order)


def solution(mesh):
    return jax.shard_map(
        on_device,
        mesh=mesh,
        in_specs=(P("win", "sta", None), P("sta", None, None), P(), P()),
        out_specs=P("sta", "win"),
        check_vma=False,
    )
```
